128 devices in a mesh: grp: 16 (over y_hi, z, core), tp: 8 (over y_lo, x).
Axes of the slice: x: 4, y: 4 (y_hi: 2, y_lo: 2; y = y_hi * 2 + y_lo), z: 4, core: 2. Of those that a mesh axis runs over, the one named last changes fastest.
Arguments:
- tokens: bfloat16 [1024, 4, 8192], P('grp', None, 'tp'), may hold values from -600 to 600
- w_qkv: bfloat16 [8192, 10240], P(('grp', 'tp')), may hold values from -0.0625 to 0.0625
- w_out: bfloat16 [8192, 8192], P(('grp', 'tp')), may hold values from -0.0625 to 0.0625
- kv_cache: bfloat16 [2048, 128, 2, 1024], P('grp', None, None, 'tp'), may hold values from -384 to 384
- row_pages: int32 [16, 64], P('grp'), may hold values from 1 to 16, 128 in all within a row
- last_fill: int32 [16, 64], P('grp'), may hold values from 1 to 128
- page_order: int32 [16, 128], P('grp'), may hold values from 0 to 127, each once within a row
Outputs:
- mixed: bfloat16 [1024, 4, 8192], P('grp', None, 'tp')
The draws below stay inside these ranges and needn't reach their ends.
Inputs may be any that keep to these rules, and one draw needn't show every extreme that they name: `row_pages`: in each group the counts sum to 128, and one count equals 16. `page_order`: each row is a permutation of the group's pool pages.
All inputs are finite; a program needn't handle non-finite values.
Results may differ from the reference program's by a relative error of at most 0.019.
Values may be sent and summed in bfloat16 or wider, within the bound.
A program may use at most 256 MiB of HBM per device.

```python
import math
import jax
import jax.numpy as jnp
import numpy as np
from jax import lax

D = 8192
HQ = 64
KVH = 8
HD = 128
STEPS = 4
BLOCK = 128
MAXP = 16
ROWS_GRP = 64
ROWS_ALL = 1024
PAGES_GRP = 128
POOL = 2048
N_GRP = 16


def draw_tokens(key, part):
    key = jax.random.fold_in(key, 11)
    key_base, key_cols, key_rows = jax.random.split(key, 3)
    shape = (ROWS_ALL, STEPS, D)
    base = jax.random.truncated_normal(key_base, -6.0, 6.0, shape, jnp.float32)
    col_scale = jnp.exp(jax.random.uniform(key_cols, (D,), jnp.float32) * math.log(10.0))
    row_scale = jnp.exp(jax.random.uniform(key_rows, (ROWS_ALL, 1, 1), jnp.float32) * math.log(10.0))
    return (base * col_scale * row_scale).astype(jnp.bfloat16)


def draw_kv_cache(key, part):
    key = jax.random.fold_in(key, 23)
    key_base = jax.random.fold_in(key, 0)
    base = jax.random.truncated_normal(key_base, -6.0, 6.0, (POOL, BLOCK, 2, KVH, HD), jnp.float32)
    return base.reshape(POOL, BLOCK, 2, KVH * HD).astype(jnp.bfloat16)


def plant(entries, key, smallest, top_value):
    dims = entries.shape
    spot = [jax.random.randint(jax.random.fold_in(key, axis), (), 0, dims[axis]) for axis in range(len(dims))]
    entries = entries.at[tuple(spot)].set(smallest)
    longest = dims.index(max(dims))
    spot[longest] = (spot[longest] + 1) % dims[longest]
    return entries.at[tuple(spot)].set(top_value)


def block_scale(own_key, shape, cuts, smallest, largest):
    gain = 1.0
    for dim, shards_of in cuts:
        draws = jax.random.uniform(jax.random.fold_in(jax.random.fold_in(own_key, 6), dim), (shards_of,), jnp.float32, smallest / len(cuts), largest / len(cuts))
        gain = gain * jnp.repeat(jnp.exp(draws), shape[dim] // shards_of).reshape((-1,) + (1,) * (len(shape) - 1 - dim))
    return gain


def profile(amount, total, reach, skew):
    weights = [(1 << 20) // math.isqrt(standing ** skew) + 1 for standing in range(2, amount + 1)]
    rest, holding = total - reach - (amount - 1), [1] * (amount - 1)
    while rest > 0:
        free = [i for i in range(amount - 1) if holding[i] < reach]
        pool, budget = sum([weights[i] for i in free]), rest
        for i in free:
            more = min(reach - holding[i], max(1, budget * weights[i] // pool), rest)
            holding[i] = holding[i] + more
            rest = rest - more
    return np.array([reach] + holding)


def ragged(own_key, number_of, total, most, skew):
    if number_of == 2:
        one = jax.random.randint(own_key, (), max(1, total - most), min(most, total - 1) + 1)
        return jnp.stack([one, total - one])
    sizes = jnp.asarray(profile(number_of, total, most, skew), jnp.int32)
    twos = (number_of - 1) // 2
    giver, receiver = sizes[1:1 + 2 * twos:2], sizes[2:2 + 2 * twos:2]
    margin = jnp.minimum(giver - 1, most - receiver)
    moved = jax.random.randint(jax.random.fold_in(own_key, 1), (twos,), 0, 1 << 20) % (margin + 1)
    sizes = sizes.at[1:1 + 2 * twos:2].set(giver - moved).at[2:2 + 2 * twos:2].set(receiver + moved)
    return sizes[jax.random.permutation(jax.random.fold_in(own_key, 2), number_of)]


def gaussian(own_key, dims, deviation, reach, cuts=(), kind=jnp.bfloat16):
    values = deviation * jax.random.normal(own_key, dims, jnp.float32)
    if cuts:
        values = values * block_scale(own_key, dims, cuts, -0.22, 0.18)
    return jnp.clip(values, -reach, reach).astype(kind)


def setup_inputs(seed: int = 0) -> dict:
    arg_keys = jax.random.split(jax.random.key(seed), 8)
    tokens = draw_tokens(jax.random.fold_in(arg_keys[7], 71), 0)
    w_qkv = gaussian(arg_keys[1], (D, (HQ + 2 * KVH) * HD), D ** -0.5, 0.0625, ((0, 128),))
    w_out = gaussian(arg_keys[2], (D, HQ * HD), (HQ * HD) ** -0.5, 0.0625, ((0, 128),))
    kv_cache = draw_kv_cache(jax.random.fold_in(arg_keys[7], 71), 0)
    row_pages = jax.vmap(lambda own: ragged(own, ROWS_GRP, PAGES_GRP, MAXP, 2))(jax.random.split(arg_keys[4], N_GRP)).reshape((N_GRP, ROWS_GRP)).astype(jnp.int32)
    last_fill = plant(jax.random.randint(arg_keys[5], (N_GRP, ROWS_GRP), 1, BLOCK + 1), jax.random.fold_in(arg_keys[5], 1), 1, BLOCK).astype(jnp.int32)
    page_order = jax.vmap(lambda own: jax.random.permutation(own, PAGES_GRP))(jax.random.split(arg_keys[6], N_GRP)).reshape((N_GRP, PAGES_GRP)).astype(jnp.int32)
    return {"tokens": tokens, "w_qkv": w_qkv, "w_out": w_out, "kv_cache": kv_cache, "row_pages": row_pages, "last_fill": last_fill, "page_order": page_order}


epsilon = 1e-05

def reference(tokens, w_qkv, w_out, kv_cache, row_pages, last_fill, page_order):
    total_rows, step_count, width = tokens.shape
    widened = tokens.astype(jnp.float32)
    normed = (widened * lax.rsqrt(lax.optimization_barrier(jnp.mean(widened * widened, axis=2, keepdims=True)) + epsilon)).astype(jnp.bfloat16)
    projected = jnp.dot(normed.reshape(-1, width), w_qkv, preferred_element_type=jnp.float32).astype(jnp.bfloat16)
    per_group = HQ // KVH
    qkv_all = projected.reshape(total_rows, step_count, KVH, per_group + 2, HD)
    queries = qkv_all[:, :, :, :per_group]
    new_key = qkv_all[:, :, :, per_group]
    new_value = qkv_all[:, :, :, per_group + 1]
    page_counts = row_pages.reshape(-1)
    lengths = (page_counts - 1) * BLOCK + last_fill.reshape(-1)
    row_starts = (jnp.cumsum(row_pages, axis=1) - row_pages).reshape(-1).astype(jnp.int32)
    groups = (jnp.arange(total_rows, dtype=jnp.int32) // ROWS_GRP).astype(jnp.int32)
    cache_view = kv_cache.reshape(POOL, BLOCK, 2, KVH, HD)
    flat_order = page_order.reshape(-1)
    score_scale = HD ** (-0.5)

    def one_row(packed):
        query_row, key_row, value_row, row_start, row_length, group_id = packed
        slot_index = jnp.minimum(row_start + jnp.arange(MAXP, dtype=jnp.int32), PAGES_GRP - 1).astype(jnp.int32)
        page_ids = flat_order[group_id * PAGES_GRP + slot_index] + group_id * PAGES_GRP
        gathered = cache_view[page_ids].reshape(MAXP * BLOCK, 2, KVH, HD)
        cache_keys = gathered[:, 0].astype(jnp.float32)
        cache_vals = gathered[:, 1].astype(jnp.float32)
        query_f = query_row.astype(jnp.float32)
        cache_scores = jnp.einsum('skgd,tkd->kgst', query_f, cache_keys, precision=lax.Precision.HIGHEST) * score_scale
        live_mask = jnp.arange(MAXP * BLOCK, dtype=jnp.int32) < row_length
        cache_scores = jnp.where(live_mask, cache_scores, -jnp.inf)
        new_scores = jnp.einsum('skgd,ukd->kgsu', query_f, key_row.astype(jnp.float32), precision=lax.Precision.HIGHEST) * score_scale
        causal = jnp.arange(step_count)[:, None] >= jnp.arange(step_count)[None, :]
        new_scores = jnp.where(causal, new_scores, -jnp.inf)
        row_top = jnp.maximum(lax.optimization_barrier(jnp.max(cache_scores, axis=-1)), lax.optimization_barrier(jnp.max(new_scores, axis=-1)))
        cache_prob = jnp.where(live_mask, jnp.exp(cache_scores - row_top[..., None]), 0.0)
        new_prob = jnp.where(causal, jnp.exp(new_scores - row_top[..., None]), 0.0)
        row_total = lax.optimization_barrier(jnp.sum(cache_prob, axis=-1)) + lax.optimization_barrier(jnp.sum(new_prob, axis=-1))
        cache_weight = (cache_prob / row_total[..., None]).astype(jnp.bfloat16).astype(jnp.float32)
        new_weight = (new_prob / row_total[..., None]).astype(jnp.bfloat16).astype(jnp.float32)
        context = jnp.einsum('kgst,tkd->skgd', cache_weight, cache_vals, precision=lax.Precision.HIGHEST)
        context = context + jnp.einsum('kgsu,ukd->skgd', new_weight, value_row.astype(jnp.float32), precision=lax.Precision.HIGHEST)
        return context.astype(jnp.bfloat16)
    context_all = lax.map(one_row, (queries, new_key, new_value, row_starts, lengths, groups))
    mixed = jnp.dot(context_all.reshape(total_rows * step_count, HQ * HD), w_out.T, preferred_element_type=jnp.float32)
    return mixed.astype(jnp.bfloat16).reshape(total_rows, step_count, width)
```

```python
import functools

import jax
import jax.numpy as jnp
from jax import lax
from jax.experimental import pallas as pl
from jax.experimental.pallas import tpu as pltpu
from jax.sharding import PartitionSpec as P

HD = 128
STEPS = 4
PER_GROUP = 8
BLOCK = 128
ROWS = 64
PAGES = 128
TOK = ROWS * STEPS
D = 8192
TP = 8
QC = 1280
OC = 1024
EPS = 1e-05
SCALE = HD ** (-0.5)
MESH = pl.DeviceIdType.MESH
NEG = -1e30
MIB = 1 << 20


def page_tables(row_pages, last_fill, row_of, valid_of, first_of, last_of):
    def rows(r, end):
        end = end + row_pages[r]
        last_of[r] = end - 1
        return end

    lax.fori_loop(0, ROWS, rows, jnp.int32(0))

    def slots(i, carry):
        r, j = carry
        pages = row_pages[r]
        row_of[i] = r
        first_of[i] = j
        valid_of[i] = jnp.where(j == pages - 1, last_fill[r], BLOCK)
        done = j + 1 == pages
        return (
            jnp.minimum(jnp.where(done, r + 1, r), ROWS - 1),
            jnp.where(done, 0, j + 1),
        )

    lax.fori_loop(0, PAGES, slots, (jnp.int32(0), jnp.int32(0)))


def new_tokens(proj, q_ref, m_new, l_new, o_new):
    def group(g, _):
        base = pl.multiple_of(g * 16, 16)
        heads = [
            proj[pl.ds(base, 16), pl.ds(a * HD, HD)].astype(jnp.float32)
            for a in range(PER_GROUP)
        ]
        for r in range(4):
            q_ref[g * 4 + r] = jnp.concatenate(
                [h[4 * r : 4 * r + 4] for h in heads], axis=0
            ).astype(jnp.bfloat16)
        key = proj[pl.ds(base, 16), pl.ds(PER_GROUP * HD, HD)]
        value = proj[pl.ds(base, 16), pl.ds((PER_GROUP + 1) * HD, HD)]
        q = q_ref[pl.ds(g * 4, 4)].reshape(128, HD)
        s = (
            lax.dot_general(
                q, key, (((1,), (1,)), ((), ())), preferred_element_type=jnp.float32
            )
            * SCALE
        )
        i = lax.broadcasted_iota(jnp.int32, s.shape, 0)
        j = lax.broadcasted_iota(jnp.int32, s.shape, 1)
        live = ((i >> 5) == (j >> 2)) & ((j & 3) <= (i & 3))
        s = jnp.where(live, s, -jnp.inf)
        m = jnp.max(s, axis=1, keepdims=True)
        p = jnp.exp(s - m)
        total = jnp.sum(p, axis=1, keepdims=True)
        o = jnp.dot(p.astype(jnp.bfloat16), value, preferred_element_type=jnp.float32)
        m_new[pl.ds(g * 4, 4)] = jnp.broadcast_to(m, (128, HD)).reshape(4, 32, HD)
        l_new[pl.ds(g * 4, 4)] = jnp.broadcast_to(total, (128, HD)).reshape(4, 32, HD)
        o_new[pl.ds(g * 4, 4)] = o.reshape(4, 32, HD)
        return 0

    lax.fori_loop(0, ROWS // 4, group, 0)


def cached_tokens(order, cache, q_ref, row_of, valid_of, m_pg, l_pg, o_pg):
    lane = lax.broadcasted_iota(jnp.int32, (32, 2 * BLOCK), 1)
    even = (lane & 1) == 0

    def some(n, _):
        for k in range(8):
            i = n * 8 + k
            kv = cache[order[i]]
            q = q_ref[row_of[i]]
            s = (
                lax.dot_general(
                    q, kv, (((1,), (1,)), ((), ())), preferred_element_type=jnp.float32
                )
                * SCALE
            )
            s = jnp.where(even & (lane < 2 * valid_of[i]), s, -jnp.inf)
            m = jnp.max(s, axis=1, keepdims=True)
            p = jnp.exp(s - m)
            total = jnp.sum(p, axis=1, keepdims=True)
            w = pltpu.roll(p, 1, 1).astype(jnp.bfloat16)
            o_pg[i] = jnp.dot(w, kv, preferred_element_type=jnp.float32)
            m_pg[i] = jnp.broadcast_to(m, (32, HD))
            l_pg[i] = jnp.broadcast_to(total, (32, HD))
        return 0

    lax.fori_loop(0, PAGES // 8, some, 0)


def join_pages(row_of, first_of, last_of, new, pg, ctx):
    m_new, l_new, o_new = new
    m_pg, l_pg, o_pg = pg

    def slot(i, run):
        r = row_of[i]
        first = first_of[i] == 0
        m0 = jnp.where(first, m_new[r], run[0])
        l0 = jnp.where(first, l_new[r], run[1])
        o0 = jnp.where(first, o_new[r], run[2])
        m1 = m_pg[i]
        m = jnp.maximum(m0, m1)
        a0 = jnp.exp(m0 - m)
        a1 = jnp.exp(m1 - m)
        total = l0 * a0 + l_pg[i] * a1
        o = o0 * a0 + o_pg[i] * a1
        l_pg[i] = total
        o_pg[i] = o
        return m, total, o

    zero = jnp.zeros((32, HD), jnp.float32)
    lax.fori_loop(0, PAGES, slot, (zero, zero, zero))

    def group(g, _):
        rows = []
        for r in range(4):
            i = last_of[g * 4 + r]
            rows.append(o_pg[i] / l_pg[i])
        for a in range(PER_GROUP):
            ctx[pl.ds(pl.multiple_of(g * 16, 16), 16), pl.ds(a * HD, HD)] = jnp.concatenate(
                [o[4 * a : 4 * a + 4] for o in rows], axis=0
            ).astype(jnp.bfloat16)
        return 0

    lax.fori_loop(0, ROWS // 4, group, 0)


def attention_kernel(
    row_pages, last_fill, order, proj, cache_hbm, ctx,
    cache, q_ref, m_new, l_new, o_new, m_pg, l_pg, o_pg,
    row_of, valid_of, first_of, last_of, sems,
):
    def part(n):
        rows = pl.ds(n * 16, 16)
        return pltpu.make_async_copy(cache_hbm.at[rows], cache.at[rows], sems.at[n])

    for n in range(8):
        part(n).start()
    page_tables(row_pages, last_fill, row_of, valid_of, first_of, last_of)
    new_tokens(proj, q_ref, m_new, l_new, o_new)
    for n in range(8):
        part(n).wait()
    cached_tokens(order, cache, q_ref, row_of, valid_of, m_pg, l_pg, o_pg)
    join_pages(row_of, first_of, last_of, (m_new, l_new, o_new), (m_pg, l_pg, o_pg), ctx)


def attention_scratch():
    f32 = jnp.float32
    return [
        pltpu.VMEM((PAGES, 2 * BLOCK, HD), jnp.bfloat16),
        pltpu.VMEM((ROWS, 32, HD), jnp.bfloat16),
        pltpu.VMEM((ROWS, 32, HD), f32),
        pltpu.VMEM((ROWS, 32, HD), f32),
        pltpu.VMEM((ROWS, 32, HD), f32),
        pltpu.VMEM((PAGES, 32, HD), f32),
        pltpu.VMEM((PAGES, 32, HD), f32),
        pltpu.VMEM((PAGES, 32, HD), f32),
        pltpu.SMEM((PAGES,), jnp.int32),
        pltpu.SMEM((PAGES,), jnp.int32),
        pltpu.SMEM((PAGES,), jnp.int32),
        pltpu.SMEM((ROWS,), jnp.int32),
    ]


def attention(row_pages, last_fill, order, proj, cache):
    smem = pl.BlockSpec(memory_space=pltpu.SMEM)
    return pl.pallas_call(
        attention_kernel,
        out_shape=jax.ShapeDtypeStruct((TOK, OC), jnp.bfloat16),
        in_specs=[smem, smem, smem, pl.BlockSpec(memory_space=pltpu.VMEM), pl.BlockSpec(memory_space=pl.ANY)],
        out_specs=pl.BlockSpec(memory_space=pltpu.VMEM),
        scratch_shapes=attention_scratch() + [pltpu.SemaphoreType.DMA((8,))],
        compiler_params=pltpu.CompilerParams(vmem_limit_bytes=40 * MIB),
        name="attention",
    )(row_pages, last_fill, order, proj, cache)


class Place:
    def __init__(self):
        g, t = lax.axis_index("grp"), lax.axis_index("tp")
        self.g, self.t = g, t
        self.core = g % 2
        self.z = (g // 2) % 4
        self.yh = g // 8
        self.yl = t // 4
        self.x = t % 4
        self.s = self.yh * TP + t
        self.zm = (self.z + 3) % 4
        self.zp = (self.z + 1) % 4
        self.z2 = (self.z + 2) % 4

    def grp(self, yh, z, core):
        return (yh * 4 + z) * 2 + core

    def plane(self, k):
        s = (self.s + k) % 16
        return self.grp(s // TP, self.z, self.core), s % TP

    def above(self):
        return self.grp(self.yh, self.zp, self.core), self.t

    def below(self):
        return self.grp(self.yh, self.zm, self.core), self.t

    def other(self):
        return self.grp(self.yh, self.z, 1 - self.core), self.t


def greet(me, extra):
    barrier = pltpu.get_barrier_semaphore()

    def one(k, _):
        pl.semaphore_signal(barrier, inc=1, device_id=me.plane(k), device_id_type=MESH)
        return 0

    lax.fori_loop(1, 16, one, 0)
    for who in extra:
        pl.semaphore_signal(barrier, inc=1, device_id=who, device_id_type=MESH)
    pl.semaphore_wait(barrier, 15 + len(extra))


class Weights:
    def __init__(self, me, w, buf, width, own, sent, up, down, got):
        self.me, self.w, self.buf, self.width = me, w, buf, width
        self.own_sem, self.sent, self.up, self.down, self.got = own, sent, up, down, got

    def columns(self, t):
        return self.w.at[:, pl.ds(pl.multiple_of(t * self.width, self.width), self.width)]

    def own(self):
        me = self.me
        return pltpu.make_async_copy(self.columns(me.t), self.buf.at[me.z, me.s], self.own_sem.at[0])

    def to_plane(self, k):
        me = self.me
        who = me.plane(k)
        return pltpu.make_async_remote_copy(
            self.columns(who[1]), self.buf.at[me.z, me.s],
            self.sent.at[k], self.got.at[me.z, me.s],
            device_id=who, device_id_type=MESH,
        )

    def along(self, z, s, who, sem):
        slot = self.buf.at[z, s]
        return pltpu.make_async_remote_copy(
            slot, slot, sem, self.got.at[z, s], device_id=who, device_id_type=MESH
        )

    def send_up(self, z, s, k):
        return self.along(z, s, self.me.above(), self.up.at[k])

    def send_down(self, z, s, k):
        return self.along(z, s, self.me.below(), self.down.at[k])

    def source(self, k):
        return (self.me.s + 16 - k) % 16

    def start(self):
        def one(k, _):
            self.to_plane(k).start()
            return 0

        self.own().start()
        lax.fori_loop(1, 16, one, 0)

    def pass_own(self):
        me = self.me
        self.own().wait()
        self.send_up(me.z, me.s, 0).start()
        self.send_down(me.z, me.s, 0).start()

        def one(k, _):
            s = self.source(k)
            self.along(me.z, s, me.above(), self.up.at[k]).wait_recv()
            self.send_up(me.z, s, k).start()
            self.send_down(me.z, s, k).start()
            return 0

        lax.fori_loop(1, 16, one, 0)

    def pass_on(self):
        me = self.me

        def got(z, k):
            self.along(z, self.source(k), me.above(), self.up.at[0]).wait_recv()

        def two(n, _):
            k = 2 * n
            got(me.zm, k)
            self.send_up(me.zm, self.source(k), 16 + n).start()
            got(me.zp, k)
            got(me.zp, k + 1)
            self.send_down(me.zp, self.source(k + 1), 16 + n).start()
            got(me.zm, k + 1)
            return 0

        lax.fori_loop(0, 8, two, 0)

    def last(self):
        me = self.me

        def one(k, _):
            self.along(me.z2, self.source(k), me.above(), self.up.at[0]).wait_recv()
            return 0

        lax.fori_loop(0, 16, one, 0)

    def finish(self):
        me = self.me

        def plane(k, _):
            self.to_plane(k).wait_send()
            return 0

        lax.fori_loop(1, 16, plane, 0)

        def ring(k, _):
            self.send_up(me.z, k % 16, k).wait_send()
            self.send_down(me.z, k % 16, k).wait_send()
            return 0

        lax.fori_loop(0, 24, ring, 0)


def weight_sems():
    dma = pltpu.SemaphoreType.DMA
    return [dma((1,)), dma((16,)), dma((24,)), dma((24,)), dma((4, 16))]


def project_kernel(
    tok, w, out,
    xbuf, wbuf, acc, squares, acc_in, squares_in,
    own, sent, up, down, got,
    x_own, x_sent, x_up, x_down, x_got, last_sent, last_got,
):
    me = Place()
    c = me.core
    side = (me.grp(me.yh, me.z, c), (1 - me.yl) * 4 + me.x)
    cross = (me.grp(me.yh, me.z, 1 - c), (1 - me.yl) * 4 + me.x)
    other = me.other()
    right = (me.g, me.yl * 4 + (me.x + 1) % 4)
    left = (me.g, me.yl * 4 + (me.x + 3) % 4)
    greet(me, (me.above(), me.below(), other, cross))

    def half(h):
        return tok.at[:, pl.ds(pl.multiple_of(h * 512, 512), 512)]

    x_own_copy = pltpu.make_async_copy(half(c), xbuf.at[me.t, c], x_own.at[0])
    x_own_copy.start()

    def x_send(n, who, h):
        return pltpu.make_async_remote_copy(
            half(h), xbuf.at[me.t, c], x_sent.at[n], x_got.at[me.t, c],
            device_id=who, device_id_type=MESH,
        )

    firsts = [x_send(0, other, 1 - c), x_send(1, side, c), x_send(2, cross, 1 - c)]
    for copy in firsts:
        copy.start()
    weights = Weights(me, w, wbuf, QC, own, sent, up, down, got)
    weights.start()

    def x_along(t, h, who, sem):
        slot = xbuf.at[t, h]
        return pltpu.make_async_remote_copy(
            slot, slot, sem, x_got.at[t, h], device_id=who, device_id_type=MESH
        )

    t_side = (1 - me.yl) * 4 + me.x
    x_own_copy.wait()
    pieces = [(me.t, c), (me.t, 1 - c), (t_side, c), (t_side, 1 - c)]
    for n, (t, h) in enumerate(pieces):
        if n:
            x_along(t, h, right, x_up.at[0]).wait_recv()
        x_along(t, h, right, x_up.at[n]).start()
        x_along(t, h, left, x_down.at[n]).start()

    weights.pass_own()

    xl, xr, x2 = (me.x + 3) % 4, (me.x + 1) % 4, (me.x + 2) % 4
    for yl in range(2):
        for h in range(2):
            x_along(yl * 4 + xl, h, right, x_up.at[0]).wait_recv()
            x_along(yl * 4 + xr, h, right, x_up.at[0]).wait_recv()
        x_along(yl * 4 + xl, 0, right, x_up.at[4 + yl]).start()
        x_along(yl * 4 + xr, 1, left, x_down.at[4 + yl]).start()

    acc[...] = jnp.zeros_like(acc)
    squares[...] = jnp.zeros_like(squares)

    def multiply(z):
        def tile(n, _):
            cols = pl.ds(pl.multiple_of(n * 256, 256), 256)
            total = acc[:, cols]
            for yh in range(2):
                xs = xbuf[yh * 4 + z].reshape(2 * TOK, 512)
                ws = wbuf[z, pl.ds(yh * 8, 8), :, cols].reshape(512, 256)
                total = total + jnp.dot(xs, ws, preferred_element_type=jnp.float32)
            acc[:, cols] = total
            return 0

        lax.fori_loop(0, QC // 256, tile, 0)

    for yl in range(2):
        for h in range(2):
            x_along(yl * 4 + x2, h, right, x_up.at[0]).wait_recv()

    weights.pass_on()
    multiply(me.z)

    def square(n, _):
        t, r = n // 8, n % 8
        rows = pl.ds(pl.multiple_of((r % 4) * 64, 64), 64)
        v = xbuf[t, r // 4, rows, :].astype(jnp.float32)
        v = v * v
        where = pl.ds(pl.multiple_of(r * 64, 64), 64)
        squares[where, :] += v[:, :128] + v[:, 128:256] + v[:, 256:384] + v[:, 384:]
        return 0

    lax.fori_loop(0, 64, square, 0)
    multiply(me.zm)
    multiply(me.zp)
    weights.last()
    multiply(me.z2)

    mine = pl.ds(pl.multiple_of(c * TOK, TOK), TOK)
    theirs = pl.ds(pl.multiple_of((1 - c) * TOK, TOK), TOK)
    swaps = [
        pltpu.make_async_remote_copy(
            acc.at[theirs], acc_in, last_sent.at[0], last_got.at[0],
            device_id=other, device_id_type=MESH,
        ),
        pltpu.make_async_remote_copy(
            squares.at[theirs], squares_in, last_sent.at[1], last_got.at[1],
            device_id=other, device_id_type=MESH,
        ),
    ]
    for copy in swaps:
        copy.start()
    for copy in firsts:
        copy.wait_send()
    for n in range(6):
        x_along(me.t, c, right, x_up.at[n]).wait_send()
        x_along(me.t, c, left, x_down.at[n]).wait_send()
    weights.finish()
    for copy in swaps:
        copy.wait()
    mean = jnp.sum(squares[mine, :] + squares_in[...], axis=1, keepdims=True) * (1.0 / D)
    gain = lax.rsqrt(mean + EPS)

    def scale(n, _):
        cols = pl.ds(pl.multiple_of(n * 256, 256), 256)
        out[:, cols] = ((acc[mine, cols] + acc_in[:, cols]) * gain).astype(jnp.bfloat16)
        return 0

    lax.fori_loop(0, QC // 256, scale, 0)


def project(tokens, w):
    dma = pltpu.SemaphoreType.DMA
    anywhere = pl.BlockSpec(memory_space=pl.ANY)
    return pl.pallas_call(
        project_kernel,
        out_shape=jax.ShapeDtypeStruct((TOK, QC), jnp.bfloat16),
        in_specs=[anywhere, anywhere],
        out_specs=pl.BlockSpec(memory_space=pltpu.VMEM),
        scratch_shapes=[
            pltpu.VMEM((TP, 2, TOK, 512), jnp.bfloat16),
            pltpu.VMEM((4, 16, 64, QC), jnp.bfloat16),
            pltpu.VMEM((2 * TOK, QC), jnp.float32),
            pltpu.VMEM((2 * TOK, 128), jnp.float32),
            pltpu.VMEM((TOK, QC), jnp.float32),
            pltpu.VMEM((TOK, 128), jnp.float32),
        ]
        + weight_sems()
        + [dma((1,)), dma((3,)), dma((6,)), dma((6,)), dma((TP, 2)), dma((2,)), dma((2,))],
        compiler_params=pltpu.CompilerParams(
            collective_id=0, has_side_effects=True, vmem_limit_bytes=48 * MIB
        ),
        cost_estimate=pl.CostEstimate(
            flops=2 * TOK * D * QC, bytes_accessed=64 * QC * 2, transcendentals=0
        ),
        name="project",
    )(tokens, w)


def output_kernel(
    ctx, w, out,
    cbuf, wbuf, part, terms, edge, edge_in,
    own, sent, up, down, got,
    c_sem, c_got, t_sent, t_got, last_sent, last_got,
):
    me = Place()
    c = me.core
    other = me.other()
    greet(me, (me.above(), me.below(), other))
    weights = Weights(me, w, wbuf, OC, own, sent, up, down, got)
    mine = pltpu.make_async_copy(ctx, cbuf.at[c], c_sem.at[0])
    swap = pltpu.make_async_remote_copy(
        ctx, cbuf.at[c], c_sem.at[1], c_got.at[0], device_id=other, device_id_type=MESH
    )
    mine.start()
    swap.start()
    weights.start()
    weights.pass_own()
    mine.wait()
    swap.wait()

    def give(t):
        return pltpu.make_async_remote_copy(
            part.at[t], terms.at[me.t], t_sent.at[t], t_got.at[me.t],
            device_id=(me.g, t), device_id_type=MESH,
        )

    def multiply(z):
        for yh in range(2):
            t = yh * 4 + z
            xs = cbuf[...].reshape(2 * TOK, OC)

            def tile(n, _, yh=yh, t=t, xs=xs):
                ws = wbuf[z, pl.ds(yh * 8 + n * 4, 4)].reshape(256, OC)
                part[t, :, pl.ds(pl.multiple_of(n * 256, 256), 256)] = lax.dot_general(
                    xs, ws, (((1,), (1,)), ((), ())), preferred_element_type=jnp.float32
                ).astype(jnp.bfloat16)
                return 0

            lax.fori_loop(0, 2, tile, 0)

            @pl.when(t != me.t)
            def _(t=t):
                give(t).start()

    weights.pass_on()
    multiply(me.z)
    multiply(me.zm)
    multiply(me.zp)
    weights.last()
    multiply(me.z2)

    def arrive(k, _):
        t = (me.t + k) % TP
        pltpu.make_async_remote_copy(
            part.at[t], terms.at[t], t_sent.at[t], t_got.at[t],
            device_id=(me.g, t), device_id_type=MESH,
        ).wait()
        return 0

    lax.fori_loop(1, TP, arrive, 0)

    def add(n, _):
        rows = pl.ds(pl.multiple_of(n * 64, 64), 64)
        total = part[me.t, rows, :].astype(jnp.float32)
        for k in range(1, TP):
            total = total + terms[(me.t + k) % TP, rows, :].astype(jnp.float32)
        edge[n // 4, pl.ds(pl.multiple_of((n % 4) * 64, 64), 64), :] = total.astype(jnp.bfloat16)
        return 0

    lax.fori_loop(0, 8, add, 0)
    back = pltpu.make_async_remote_copy(
        edge.at[1 - c], edge_in, last_sent.at[0], last_got.at[0],
        device_id=other, device_id_type=MESH,
    )
    back.start()
    weights.finish()
    out[:, pl.ds(pl.multiple_of(c * 512, 512), 512)] = edge[c]
    back.wait()
    out[:, pl.ds(pl.multiple_of((1 - c) * 512, 512), 512)] = edge_in[...]


def output(ctx, w):
    dma = pltpu.SemaphoreType.DMA
    anywhere = pl.BlockSpec(memory_space=pl.ANY)
    bf16 = jnp.bfloat16
    return pl.pallas_call(
        output_kernel,
        out_shape=jax.ShapeDtypeStruct((TOK, OC), bf16),
        in_specs=[anywhere, anywhere],
        out_specs=pl.BlockSpec(memory_space=pltpu.VMEM),
        scratch_shapes=[
            pltpu.VMEM((2, TOK, OC), bf16),
            pltpu.VMEM((4, 16, 64, OC), bf16),
            pltpu.VMEM((TP, 2 * TOK, 512), bf16),
            pltpu.VMEM((TP, 2 * TOK, 512), bf16),
            pltpu.VMEM((2, TOK, 512), bf16),
            pltpu.VMEM((TOK, 512), bf16),
        ]
        + weight_sems()
        + [dma((2,)), dma((1,)), dma((TP,)), dma((TP,)), dma((1,)), dma((1,))],
        compiler_params=pltpu.CompilerParams(
            collective_id=1, has_side_effects=True, vmem_limit_bytes=48 * MIB
        ),
        cost_estimate=pl.CostEstimate(
            flops=2 * TOK * D * OC, bytes_accessed=64 * OC * 2, transcendentals=0
        ),
        name="output",
    )(ctx, w)


def per_device(tokens, w_qkv, w_out, kv_cache, row_pages, last_fill, page_order):
    projected = project(tokens.reshape(TOK, -1), w_qkv)
    context = attention(
        row_pages.reshape(-1), last_fill.reshape(-1), page_order.reshape(-1),
        projected, kv_cache.reshape(PAGES, 2 * BLOCK, HD),
    )
    return output(context, w_out).reshape(ROWS, STEPS, -1)


def solution(mesh):
    placed = (
        P("grp", None, "tp"),
        P(("grp", "tp"), None),
        P(("grp", "tp"), None),
        P("grp", None, None, "tp"),
        P("grp", None),
        P("grp", None),
        P("grp", None),
    )
    return jax.shard_map(
        per_device, mesh=mesh, in_specs=placed, out_specs=P("grp", None, "tp"), check_vma=False
    )
```

```python
import jax
import jax.numpy as jnp
from jax import lax
from jax.experimental import pallas as pl
from jax.experimental.pallas import tpu as pltpu
from jax.sharding import PartitionSpec as P

HD = 128
STEPS = 4
PER_GROUP = 8
BLOCK = 128
ROWS = 64
PAGES = 128
TOK = ROWS * STEPS
D = 8192
TP = 8
QC = 1280
OC = 1024
EPS = 1e-05
SCALE = HD ** (-0.5)
MESH = pl.DeviceIdType.MESH
MIB = 1 << 20


def page_maps(row_pages, last_fill, order, of_page, of_row, valid):
    f32 = jnp.float32
    none = jnp.zeros((1, PAGES - ROWS), f32)
    pages = jnp.concatenate([row_pages[...].astype(f32), none], axis=1)
    fill = jnp.concatenate([last_fill[...].astype(f32), none], axis=1)
    down = lax.broadcasted_iota(jnp.int32, (PAGES, PAGES), 0)
    along = lax.broadcasted_iota(jnp.int32, (PAGES, PAGES), 1)
    upto = jnp.where(down <= along, 1.0, 0.0)
    end = jnp.dot(jnp.broadcast_to(pages, (8, PAGES)), upto, preferred_element_type=f32)[0:1]
    place = jnp.sum(
        jnp.where(order[...] == down, along.astype(f32), 0.0), axis=1, keepdims=True
    )
    mine = (place >= end - pages) & (place < end)
    used = jnp.where(place == end - 1.0, fill, float(BLOCK))
    valid[...] = jnp.broadcast_to(
        jnp.sum(jnp.where(mine, used, 0.0), axis=1, keepdims=True), (PAGES, PAGES)
    )
    found = jnp.where(mine, 1.0, 0.0)
    of_page[...] = found
    of_row[...] = found.T[:ROWS]


def page_queries(pf, of_page, q_pg):
    def head(a, _):
        for step in range(STEPS):
            q = pf[a, pl.ds(step, ROWS, stride=STEPS), :]
            q_pg[pl.ds(a * STEPS + step, PAGES, stride=32), :] = jnp.dot(
                of_page[:, :ROWS], q, preferred_element_type=jnp.float32
            )
        return 0

    lax.fori_loop(0, PER_GROUP, head, 0)


def cached_tokens(cache, q_pg, valid, m_all, l_all, o_pg):
    n_at = 16
    lane = lax.broadcasted_iota(jnp.int32, (1, 2 * BLOCK), 1)
    lane = jnp.where((lane & 1) == 0, lane.astype(jnp.float32), 1e6)
    page = lax.broadcasted_iota(jnp.int32, (32, PAGES), 1)

    def some(n, run):
        m_run, l_run = run
        slots = [n * n_at + k for k in range(n_at)]
        pages = [cache[i] for i in slots]
        rows = [pl.ds(pl.multiple_of(i * 32, 32), 32) for i in slots]
        raw = [
            lax.dot_general(
                q_pg[at, :].astype(jnp.bfloat16), kv, (((1,), (1,)), ((), ())),
                preferred_element_type=jnp.float32,
            )
            for at, kv in zip(rows, pages)
        ]
        ends = [valid[pl.ds(i, 1), :] * 2.0 for i in slots]
        ends = [jnp.concatenate([e, e], axis=1) for e in ends]
        raw = [s * SCALE + jnp.where(lane < e, 0.0, -jnp.inf) for s, e in zip(raw, ends)]
        tops = [jnp.max(s, axis=1, keepdims=True) for s in raw]
        probs = [jnp.exp(s - m) for s, m in zip(raw, tops)]
        totals = [jnp.sum(p, axis=1, keepdims=True) for p in probs]
        moved = [pltpu.roll(p, 1, 1).astype(jnp.bfloat16) for p in probs]
        outs = [
            jnp.dot(w, kv, preferred_element_type=jnp.float32)
            for w, kv in zip(moved, pages)
        ]
        for k, i in enumerate(slots):
            o_pg[rows[k], :] = outs[k]
            m_run = jnp.where(page == i, tops[k], m_run)
            l_run = jnp.where(page == i, totals[k], l_run)
        return m_run, l_run

    zero = jnp.zeros((32, PAGES), jnp.float32)
    m_all[...], l_all[...] = lax.fori_loop(0, PAGES // n_at, some, (zero, zero))


def join_pages(pf, of_row, m_all, l_all, o_pg, joined):
    def head(a, _):
        for step in range(STEPS):
            h = a * STEPS + step
            rows = pl.ds(step, ROWS, stride=STEPS)
            q = pf[a, rows, :]
            fresh = [
                jnp.sum(
                    q * pf[PER_GROUP, pl.ds(u, ROWS, stride=STEPS), :], axis=1, keepdims=True
                )
                * SCALE
                for u in range(step + 1)
            ]
            tops = jnp.where(of_row[...] > 0.5, m_all[pl.ds(h, 1), :], -jnp.inf)
            top = jnp.max(tops, axis=1, keepdims=True)
            for s in fresh:
                top = jnp.maximum(top, s)
            share = jnp.exp(tops - top)
            total = jnp.sum(share * l_all[pl.ds(h, 1), :], axis=1, keepdims=True)
            out = jnp.dot(
                share, o_pg[pl.ds(h, PAGES, stride=32), :],
                preferred_element_type=jnp.float32, precision=lax.Precision.HIGHEST,
            )
            for u, s in enumerate(fresh):
                p = jnp.exp(s - top)
                total = total + p
                out = out + p * pf[PER_GROUP + 1, pl.ds(u, ROWS, stride=STEPS), :]
            joined[a, rows, :] = out / total
        return 0

    lax.fori_loop(0, PER_GROUP, head, 0)


class Place:
    def __init__(self):
        g, t = lax.axis_index("grp"), lax.axis_index("tp")
        self.g, self.t = g, t
        self.core = g % 2
        self.z = (g // 2) % 4
        self.yh = g // 8
        self.yl = t // 4
        self.x = t % 4
        self.y = self.yh * 2 + self.yl
        self.zm = (self.z + 3) % 4
        self.zp = (self.z + 1) % 4
        self.z2 = (self.z + 2) % 4

    def at(self, y=None, z=None, x=None, core=None):
        y = self.y if y is None else y
        z = self.z if z is None else z
        x = self.x if x is None else x
        core = self.core if core is None else core
        return ((y // 2) * 4 + z) * 2 + core, (y % 2) * 4 + x


def greet(me):
    barrier = pltpu.get_barrier_semaphore()

    def signal(who):
        pl.semaphore_signal(barrier, inc=1, device_id=who, device_id_type=MESH)

    def plane(k, _):
        signal(me.at(y=(me.y + k // 4) % 4, x=(me.x + k) % 4))
        return 0

    lax.fori_loop(1, 16, plane, 0)
    signal(me.at(z=me.zp))
    signal(me.at(z=me.zm))
    for k in range(4):
        signal(me.at(y=(me.y + k) % 4, core=1 - me.core))
    for k in range(1, 4):
        signal(me.at(x=(me.x + k) % 4, core=1 - me.core))
    pl.semaphore_wait(barrier, 24)


def remote(src, dst, sent, got, who):
    return pltpu.make_async_remote_copy(
        src, dst, sent, got, device_id=who, device_id_type=MESH
    )


class Ring:
    def __init__(self, me, count, order, slot, up, down, got):
        self.me, self.count, self.order, self.slot = me, count, order, slot
        self.up, self.down, self.got = up, down, got

    def send_up(self, z, p, k):
        return remote(
            self.slot(z, p), self.slot(z, p), self.up.at[k], self.got.at[z, p],
            self.me.at(z=self.me.zp),
        )

    def send_down(self, z, p, k):
        return remote(
            self.slot(z, p), self.slot(z, p), self.down.at[k], self.got.at[z, p],
            self.me.at(z=self.me.zm),
        )

    def arrived(self, z, p):
        self.send_up(z, p, 0).wait_recv()

    def pass_own(self, local):
        def send(k):
            p = self.order(k)
            self.send_up(self.me.z, p, k).start()
            self.send_down(self.me.z, p, k).start()

        for k, copy in enumerate(local):
            copy.wait()
            send(k)

        def one(k, _):
            self.arrived(self.me.z, self.order(k))
            send(k)
            return 0

        lax.fori_loop(len(local), self.count, one, 0)

    def pass_on(self, low, high):
        me = self.me

        def two(n, _):
            p, q = self.order(2 * n), self.order(2 * n + 1)
            self.arrived(me.zm, p)
            self.send_up(me.zm, p, self.count + n).start()
            self.arrived(me.zp, p)
            self.arrived(me.zp, q)
            self.send_down(me.zp, q, self.count + n).start()
            self.arrived(me.zm, q)
            return 0

        lax.fori_loop(low, high, two, 0)

    def last(self):
        def one(k, _):
            self.arrived(self.me.z2, self.order(k))
            return 0

        lax.fori_loop(0, self.count, one, 0)

    def finish(self):
        def one(k, _):
            p = k % self.count
            self.send_up(self.me.z, p, k).wait_send()
            self.send_down(self.me.z, p, k).wait_send()
            return 0

        lax.fori_loop(0, self.count + self.count // 2, one, 0)


def ring_sems(count):
    dma = pltpu.SemaphoreType.DMA
    more = count + count // 2
    return [dma((count,)), dma((more,)), dma((more,)), dma((4, count))]


def layer_kernel(
    row_pages, last_fill, order, tok, w_qkv, w_out, cache_hbm, out,
    xbuf, qbuf, obuf, acc, squares, half_sent, half_got, full_sent, full_got,
    sq_half, sq_sum, sq_full,
    cache, pf, of_page, of_row, valid, q_pg, m_all, l_all, o_pg, joined,
    mine, ctx, o_acc, keep, give, taken, sums, final,
    own_sem, cache_sem,
    q_sent, q_up, q_down, q_got,
    w_sent, w_up, w_down, w_got,
    x_sent, x_up, x_down, x_got,
    sq_s, sq_g, h_s, h_g, f_s, f_g,
    c_up, c_down, c_core, c_got,
    y_s, y_g, e_s, e_g,
):
    me = Place()
    c = me.core
    other = me.at(core=1 - c)
    right, left = me.at(x=(me.x + 1) % 4), me.at(x=(me.x + 3) % 4)
    xl, xr, x2 = (me.x + 3) % 4, (me.x + 1) % 4, (me.x + 2) % 4
    far = me.at(y=(me.y + 2) % 4)
    near = me.at(y=me.yh * 2 + 1 - me.yl)
    greet(me)

    piece = me.yh * 2 + c

    def half(h):
        return tok.at[:, pl.ds(pl.multiple_of(h * 512, 512), 512)]

    def x_first(n):
        h = (c + n % 2) % 2
        who = me.at(y=me.yl * 2 + (me.yl + n // 2) % 2, core=h)
        return remote(half(h), xbuf.at[me.x, piece], x_sent.at[n], x_got.at[me.x, piece], who)

    stays = me.yh == me.yl

    x_here = pltpu.make_async_copy(half(c), xbuf.at[me.x, piece], own_sem.at[0])

    @pl.when(stays)
    def _():
        x_here.start()

    @pl.when(jnp.logical_not(stays))
    def _():
        x_first(0).start()

    for n in range(1, 4):
        x_first(n).start()

    def q_columns(t):
        return w_qkv.at[:, pl.ds(pl.multiple_of(t * QC, QC), QC)]

    def q_plane(k):
        t = (me.t + k) % TP
        return remote(q_columns(t), qbuf.at[me.z, me.t], q_sent.at[k], q_got.at[me.z, me.t], (me.g, t))

    def q_start(k, _):
        q_plane(k).start()
        return 0

    q_here = [pltpu.make_async_copy(q_columns(me.t), qbuf.at[me.z, me.t], own_sem.at[1])]
    q_here[0].start()
    lax.fori_loop(1, TP, q_start, 0)
    q_ring = Ring(
        me, TP, lambda k: (me.t + TP - k) % TP, lambda z, p: qbuf.at[z, p], q_up, q_down, q_got
    )

    def cached(n):
        rows = pl.ds(n * 16, 16)
        return pltpu.make_async_copy(cache_hbm.at[rows], cache.at[rows], cache_sem.at[n])

    for n in range(8):
        cached(n).start()

    def x_along(x, p, who, sem):
        return remote(xbuf.at[x, p], xbuf.at[x, p], sem, x_got.at[x, p], who)

    for n in range(4):
        p = (piece + n) % 4
        if n:
            x_along(me.x, p, right, x_up.at[0]).wait_recv()
        else:

            @pl.when(stays)
            def _():
                x_here.wait()

            @pl.when(jnp.logical_not(stays))
            def _():
                x_along(me.x, piece, right, x_up.at[0]).wait_recv()

        x_along(me.x, p, right, x_up.at[n]).start()
        x_along(me.x, p, left, x_down.at[n]).start()

    def w_columns(yl, n):
        return w_out.at[:, pl.ds(pl.multiple_of((yl * 4 + n) * OC, OC), OC)]

    def w_slot(z, p):
        return obuf.at[z, p // 4, p % 4]

    def w_plane(k):
        y, n = (me.y + k // 4) % 4, k % 4
        p = me.y * 4 + n
        return remote(w_columns(y % 2, n), w_slot(me.z, p), w_sent.at[k], w_got.at[me.z, p], me.at(y=y))

    def w_start(k, _):
        w_plane(k).start()
        return 0

    w_here = [
        pltpu.make_async_copy(w_columns(me.yl, n), w_slot(me.z, me.y * 4 + n), own_sem.at[2 + n])
        for n in range(4)
    ]
    for copy in w_here:
        copy.start()
    lax.fori_loop(4, 16, w_start, 0)
    w_ring = Ring(
        me, 16, lambda k: ((me.y + 4 - k // 4) % 4) * 4 + k % 4, w_slot, w_up, w_down, w_got
    )

    q_ring.pass_own(q_here)
    for n in range(4):
        x_along(xl, n, right, x_up.at[0]).wait_recv()
        x_along(xr, n, right, x_up.at[0]).wait_recv()
        if n < 2:
            x_along(xl, n, right, x_up.at[4 + n]).start()
        else:
            x_along(xr, n, left, x_down.at[2 + n]).start()
    q_ring.pass_on(0, 4)
    page_maps(row_pages, last_fill, order, of_page, of_row, valid)
    w_ring.pass_own(w_here)
    for n in range(4):
        x_along(x2, n, right, x_up.at[0]).wait_recv()

    squares[...] = jnp.zeros_like(squares)

    def square(n, _):
        x, p, r = n // 16, (n // 4) % 4, n % 4
        v = xbuf[x, p, pl.ds(pl.multiple_of(r * 64, 64), 64), :].astype(jnp.float32)
        v = v * v
        v = v[:, :128] + v[:, 128:256] + v[:, 256:384] + v[:, 384:]
        squares[p, pl.ds(pl.multiple_of(r * 64, 64), 64), :] += v
        return 0

    lax.fori_loop(0, 64, square, 0)
    sq_swap = [
        remote(squares.at[2 * n + 1 - c], sq_half.at[n], sq_s.at[n], sq_g.at[n], other)
        for n in range(2)
    ]
    for copy in sq_swap:
        copy.start()

    def product(z, n):
        cols = pl.ds(pl.multiple_of(n * 256, 256), 256)
        xs = xbuf[z].reshape(4 * TOK, 512)
        ws = qbuf[z, :, :, cols].reshape(512, 256)
        return cols, jnp.dot(xs, ws, preferred_element_type=jnp.float32)

    def multiply(z, fresh=False):
        def tile(n, _):
            cols, value = product(z, n)
            acc[:, cols] = value if fresh else acc[:, cols] + value
            return 0

        lax.fori_loop(0, QC // 256, tile, 0)

    multiply(me.z, True)
    for copy in sq_swap:
        copy.wait_recv()
    for n in range(2):
        sq_sum[n] = squares[2 * n + c] + sq_half[n]
    sq_far = remote(sq_sum.at[1 - me.yh], sq_full, sq_s.at[2], sq_g.at[2], far)
    sq_far.start()
    multiply(me.zm)
    multiply(me.zp)
    q_ring.last()

    def half_copy(n):
        return remote(half_sent.at[n], half_got.at[n], h_s.at[n], h_g.at[n], other)

    def full_copy(n):
        return remote(full_sent.at[n], full_got.at[n], f_s.at[n], f_g.at[n], far)

    def block(p):
        return pl.ds(pl.multiple_of(p * TOK, TOK), TOK)

    def last_tile(n):
        cols, value = product(me.z2, n)
        acc[:, cols] += value
        for m in range(2):
            half_sent[n, m] = acc[block(2 * m + 1 - c), cols].astype(jnp.bfloat16)
        half_copy(n).start()

    for n in range(QC // 256):
        last_tile(n)

    def join_half(n):
        cols = pl.ds(pl.multiple_of(n * 256, 256), 256)
        half_copy(n).wait_recv()
        theirs = acc[block(2 * (1 - me.yh) + c), cols] + half_got[n, 1 - me.yh].astype(jnp.float32)
        full_sent[n] = theirs.astype(jnp.bfloat16)
        full_copy(n).start()
        acc[block(piece), cols] += half_got[n, me.yh].astype(jnp.float32)

    for n in range(QC // 256):
        join_half(n)
    sq_far.wait_recv()
    mean = jnp.sum(sq_sum[me.yh] + sq_full[...], axis=1, keepdims=True) * (1.0 / D)
    gain = lax.rsqrt(mean + EPS)

    def join_full(n):
        cols = pl.ds(pl.multiple_of(n * 256, 256), 256)
        full_copy(n).wait_recv()
        total = acc[block(piece), cols] + full_got[n].astype(jnp.float32)
        total = (total * gain).astype(jnp.bfloat16).astype(jnp.float32)
        pf[2 * n], pf[2 * n + 1] = total[:, :HD], total[:, HD:]

    for n in range(QC // 256):
        join_full(n)

    page_queries(pf, of_page, q_pg)
    for n in range(8):
        cached(n).wait()
    cached_tokens(cache, q_pg, valid, m_all, l_all, o_pg)
    join_pages(pf, of_row, m_all, l_all, o_pg, joined)
    for a in range(PER_GROUP):
        mine[:, pl.ds(a * HD, HD)] = joined[a].astype(jnp.bfloat16)

    def c_along(x, core, h, sem, who):
        slot = ctx.at[x, core, h]
        return remote(slot, slot, sem, c_got.at[x, core, h], who)

    def c_first(h, sem, who):
        slot = ctx.at[me.x, c, h]
        return remote(mine.at[pl.ds(h * 128, 128)], slot, sem, c_got.at[me.x, c, h], who)

    c_here = [
        pltpu.make_async_copy(
            mine.at[pl.ds(h * 128, 128)], ctx.at[me.x, c, h], own_sem.at[6 + h]
        )
        for h in range(2)
    ]
    for h in range(2):
        c_first(h, c_up.at[h], right).start()
        c_first(h, c_down.at[h], left).start()
        c_first(h, c_core.at[h], other).start()
        c_here[h].start()
    w_ring.pass_on(0, 8)
    for h in range(2):
        c_along(xl, c, h, c_up.at[0], right).wait_recv()
        if h == 0:
            c_along(xl, c, h, c_up.at[2], right).start()
        c_along(xl, c, h, c_core.at[2 + h], other).start()
        c_along(xr, c, h, c_up.at[0], right).wait_recv()
        if h == 1:
            c_along(xr, c, h, c_down.at[2], left).start()
        c_along(xr, c, h, c_core.at[4 + h], other).start()
    for h in range(2):
        c_along(x2, c, h, c_up.at[0], right).wait_recv()
        c_along(x2, c, h, c_core.at[6 + h], other).start()
    for x in (me.x, xl, xr, x2):
        for h in range(2):
            c_along(x, 1 - c, h, c_up.at[0], right).wait_recv()
    for copy in c_here:
        copy.wait()

    def y_copy(j):
        return remote(give.at[j], taken.at[j], y_s.at[j], y_g.at[j], near)

    def features(j, z):
        def term(n, _):
            ws = obuf[z, :, n].reshape(256, OC)
            xs = ctx[n].reshape(2 * TOK, OC)
            value = lax.dot_general(
                xs, ws, (((1,), (1,)), ((), ())), preferred_element_type=jnp.float32
            )
            o_acc[...] = jnp.where(n == 0, value, o_acc[...] + value)
            return 0

        lax.fori_loop(0, 4, term, 0)
        keep[j] = o_acc[:, pl.ds(pl.multiple_of(me.yl * 128, 128), 128)]
        give[j] = o_acc[:, pl.ds(pl.multiple_of((1 - me.yl) * 128, 128), 128)].astype(jnp.bfloat16)
        y_copy(j).start()

    def e_copy(j, z, m):
        core = (c + m) % 2
        return remote(
            sums.at[j, core], final.at[c, me.x], e_s.at[j, m], e_g.at[c, me.x], me.at(x=z, core=core)
        )

    def spread(j, z):
        y_copy(j).wait_recv()
        total = keep[j] + taken[j].astype(jnp.float32)
        sums[j] = total.astype(jnp.bfloat16).reshape(2, TOK, 128)
        e_copy(j, z, 1).start()

        @pl.when(z != me.x)
        def _():
            e_copy(j, z, 0).start()

        @pl.when(z == me.x)
        def _():
            here = pltpu.make_async_copy(sums.at[j, c], final.at[c, me.x], own_sem.at[8])
            here.start()
            here.wait()

    features(0, me.z)
    features(1, me.zm)
    spread(0, me.z)
    features(2, me.zp)
    spread(1, me.zm)
    w_ring.last()
    features(3, me.z2)
    spread(2, me.zp)
    spread(3, me.z2)

    @pl.when(jnp.logical_not(stays))
    def _():
        x_first(0).wait_send()

    for n in range(1, 4):
        x_first(n).wait_send()
    for n in range(6):
        x_along(me.x, 0, right, x_up.at[n]).wait_send()
        x_along(me.x, 0, left, x_down.at[n]).wait_send()

    def q_done(k, _):
        q_plane(k).wait_send()
        return 0

    def w_done(k, _):
        w_plane(k).wait_send()
        return 0

    lax.fori_loop(1, TP, q_done, 0)
    lax.fori_loop(4, 16, w_done, 0)
    q_ring.finish()
    w_ring.finish()
    for copy in sq_swap:
        copy.wait_send()
    sq_far.wait_send()
    for n in range(QC // 256):
        half_copy(n).wait_send()
        full_copy(n).wait_send()
    for n in range(3):
        c_along(me.x, c, 0, c_up.at[n], right).wait_send()
        c_along(me.x, c, 0, c_down.at[n], left).wait_send()
    for n in range(8):
        c_along(me.x, c, 0, c_core.at[n], other).wait_send()
    for j, z in enumerate((me.z, me.zm, me.zp, me.z2)):
        y_copy(j).wait_send()
        e_copy(j, z, 1).wait_send()

        @pl.when(z != me.x)
        def _(j=j, z=z):
            e_copy(j, z, 0).wait_send()

    for k in range(8):
        core, x = (c + k // 4) % 2, (me.x + k) % 4
        if k:
            remote(final.at[core, x], final.at[core, x], e_s.at[0, 0], e_g.at[core, x], other).wait_recv()

    for core in range(2):
        for yl in range(2):
            out[:, pl.ds(core * 512 + yl * 256, 256)] = jnp.concatenate(
                [final[core, x, :, pl.ds(yl * 64, 64)] for x in range(4)], axis=1
            )


def layer(row_pages, last_fill, order, tokens, w_qkv, w_out, cache):
    dma = pltpu.SemaphoreType.DMA
    inside = pl.BlockSpec(memory_space=pltpu.VMEM)
    anywhere = pl.BlockSpec(memory_space=pl.ANY)
    f32, bf16 = jnp.float32, jnp.bfloat16
    tiles = QC // 256

    def vmem(dtype, *shape):
        return pltpu.VMEM(shape, dtype)

    return pl.pallas_call(
        layer_kernel,
        out_shape=jax.ShapeDtypeStruct((TOK, OC), bf16),
        in_specs=[inside] * 3 + [anywhere] * 4,
        out_specs=pl.BlockSpec(memory_space=pltpu.VMEM),
        scratch_shapes=[
            vmem(bf16, 4, 4, TOK, 512),
            vmem(bf16, 4, TP, 64, QC),
            vmem(bf16, 4, 4, 4, 64, OC),
            vmem(f32, 4 * TOK, QC),
            vmem(f32, 4, TOK, 128),
            vmem(bf16, tiles, 2, TOK, 256),
            vmem(bf16, tiles, 2, TOK, 256),
            vmem(bf16, tiles, TOK, 256),
            vmem(bf16, tiles, TOK, 256),
            vmem(f32, 2, TOK, 128),
            vmem(f32, 2, TOK, 128),
            vmem(f32, TOK, 128),
            vmem(bf16, PAGES, 2 * BLOCK, HD),
            vmem(f32, PER_GROUP + 2, TOK, HD),
            vmem(f32, PAGES, PAGES),
            vmem(f32, ROWS, PAGES),
            vmem(f32, PAGES, PAGES),
            vmem(f32, PAGES * 32, HD),
            vmem(f32, 32, PAGES),
            vmem(f32, 32, PAGES),
            vmem(f32, PAGES * 32, HD),
            vmem(f32, PER_GROUP, TOK, HD),
            vmem(bf16, TOK, OC),
            vmem(bf16, 4, 2, 2, 128, OC),
            vmem(f32, 2 * TOK, 256),
            vmem(f32, 4, 2 * TOK, 128),
            vmem(bf16, 4, 2 * TOK, 128),
            vmem(bf16, 4, 2 * TOK, 128),
            vmem(bf16, 4, 2, TOK, 128),
            vmem(bf16, 2, 4, TOK, 128),
            dma((9,)),
            dma((8,)),
        ]
        + ring_sems(TP)
        + ring_sems(16)
        + [dma((4,)), dma((6,)), dma((6,)), dma((4, 4))]
        + [dma((3,)), dma((3,)), dma((tiles,)), dma((tiles,)), dma((tiles,)), dma((tiles,))]
        + [dma((3,)), dma((3,)), dma((8,)), dma((4, 2, 2))]
        + [dma((4,)), dma((4,)), dma((4, 2)), dma((2, 4))],
        compiler_params=pltpu.CompilerParams(
            collective_id=0, has_side_effects=True, vmem_limit_bytes=60 * MIB
        ),
        cost_estimate=pl.CostEstimate(
            flops=2 * TOK * D * (QC + OC), bytes_accessed=16 * MIB, transcendentals=0
        ),
        name="layer",
    )(row_pages, last_fill, order, tokens, w_qkv, w_out, cache)


def per_device(tokens, w_qkv, w_out, kv_cache, row_pages, last_fill, page_order):
    mixed = layer(
        row_pages, last_fill, page_order,
        tokens.reshape(TOK, -1), w_qkv, w_out, kv_cache.reshape(PAGES, 2 * BLOCK, HD),
    )
    return mixed.reshape(ROWS, STEPS, -1)


def solution(mesh):
    placed = (
        P("grp", None, "tp"),
        P(("grp", "tp"), None),
        P(("grp", "tp"), None),
        P("grp", None, None, "tp"),
        P("grp", None),
        P("grp", None),
        P("grp", None),
    )
    return jax.shard_map(
        per_device, mesh=mesh, in_specs=placed, out_specs=P("grp", None, "tp"), check_vma=False
    )
```

```python
import jax
import jax.numpy as jnp
from jax import lax
from jax.experimental import pallas as pl
from jax.experimental.pallas import tpu as pltpu
from jax.sharding import PartitionSpec as P

HD = 128
STEPS = 4
PER_GROUP = 8
BLOCK = 128
ROWS = 64
PAGES = 128
TOK = ROWS * STEPS
D = 8192
TP = 8
QC = 1280
OC = 1024
EPS = 1e-05
SCALE = HD ** (-0.5)
MESH = pl.DeviceIdType.MESH
MIB = 1 << 20


def page_maps(row_pages, last_fill, order, of_page, of_row, valid):
    f32 = jnp.float32
    none = jnp.zeros((1, PAGES - ROWS), f32)
    pages = jnp.concatenate([row_pages[...].astype(f32), none], axis=1)
    fill = jnp.concatenate([last_fill[...].astype(f32), none], axis=1)
    down = lax.broadcasted_iota(jnp.int32, (PAGES, PAGES), 0)
    along = lax.broadcasted_iota(jnp.int32, (PAGES, PAGES), 1)
    upto = jnp.where(down <= along, 1.0, 0.0)
    end = jnp.dot(jnp.broadcast_to(pages, (8, PAGES)), upto, preferred_element_type=f32)[0:1]
    place = jnp.sum(
        jnp.where(order[...] == down, along.astype(f32), 0.0), axis=1, keepdims=True
    )
    mine = (place >= end - pages) & (place < end)
    used = jnp.where(place == end - 1.0, fill, float(BLOCK))
    valid[...] = jnp.broadcast_to(
        jnp.sum(jnp.where(mine, used, 0.0), axis=1, keepdims=True), (PAGES, PAGES)
    )
    found = jnp.where(mine, 1.0, 0.0)
    of_page[...] = found
    of_row[...] = found.T[:ROWS]


def page_queries(pf, of_page, q_pg):
    def head(a, _):
        for step in range(STEPS):
            q = pf[a, pl.ds(step, ROWS, stride=STEPS), :]
            q_pg[pl.ds(a * STEPS + step, PAGES, stride=32), :] = jnp.dot(
                of_page[:, :ROWS], q, preferred_element_type=jnp.float32
            )
        return 0

    lax.fori_loop(0, PER_GROUP, head, 0)


def cached_tokens(cache, q_pg, valid, m_all, l_all, o_pg):
    n_at = 16
    lane = lax.broadcasted_iota(jnp.int32, (1, 2 * BLOCK), 1)
    lane = jnp.where((lane & 1) == 0, lane.astype(jnp.float32), 1e6)
    page = lax.broadcasted_iota(jnp.int32, (32, PAGES), 1)

    def some(n, run):
        m_run, l_run = run
        slots = [n * n_at + k for k in range(n_at)]
        pages = [cache[i] for i in slots]
        rows = [pl.ds(pl.multiple_of(i * 32, 32), 32) for i in slots]
        raw = [
            lax.dot_general(
                q_pg[at, :].astype(jnp.bfloat16), kv, (((1,), (1,)), ((), ())),
                preferred_element_type=jnp.float32,
            )
            for at, kv in zip(rows, pages)
        ]
        ends = [valid[pl.ds(i, 1), :] * 2.0 for i in slots]
        ends = [jnp.concatenate([e, e], axis=1) for e in ends]
        raw = [s * SCALE + jnp.where(lane < e, 0.0, -jnp.inf) for s, e in zip(raw, ends)]
        tops = [jnp.max(s, axis=1, keepdims=True) for s in raw]
        probs = [jnp.exp(s - m) for s, m in zip(raw, tops)]
        totals = [jnp.sum(p, axis=1, keepdims=True) for p in probs]
        moved = [pltpu.roll(p, 1, 1).astype(jnp.bfloat16) for p in probs]
        outs = [
            jnp.dot(w, kv, preferred_element_type=jnp.float32)
            for w, kv in zip(moved, pages)
        ]
        for k, i in enumerate(slots):
            o_pg[rows[k], :] = outs[k]
            m_run = jnp.where(page == i, tops[k], m_run)
            l_run = jnp.where(page == i, totals[k], l_run)
        return m_run, l_run

    zero = jnp.zeros((32, PAGES), jnp.float32)
    m_all[...], l_all[...] = lax.fori_loop(0, PAGES // n_at, some, (zero, zero))


def join_pages(pf, of_row, m_all, l_all, o_pg, joined):
    def head(a, _):
        for step in range(STEPS):
            h = a * STEPS + step
            rows = pl.ds(step, ROWS, stride=STEPS)
            q = pf[a, rows, :]
            fresh = [
                jnp.sum(
                    q * pf[PER_GROUP, pl.ds(u, ROWS, stride=STEPS), :], axis=1, keepdims=True
                )
                * SCALE
                for u in range(step + 1)
            ]
            tops = jnp.where(of_row[...] > 0.5, m_all[pl.ds(h, 1), :], -jnp.inf)
            top = jnp.max(tops, axis=1, keepdims=True)
            for s in fresh:
                top = jnp.maximum(top, s)
            share = jnp.exp(tops - top)
            total = jnp.sum(share * l_all[pl.ds(h, 1), :], axis=1, keepdims=True)
            out = jnp.dot(
                share, o_pg[pl.ds(h, PAGES, stride=32), :],
                preferred_element_type=jnp.float32, precision=lax.Precision.HIGHEST,
            )
            for u, s in enumerate(fresh):
                p = jnp.exp(s - top)
                total = total + p
                out = out + p * pf[PER_GROUP + 1, pl.ds(u, ROWS, stride=STEPS), :]
            joined[a, rows, :] = out / total
        return 0

    lax.fori_loop(0, PER_GROUP, head, 0)


class Place:
    def __init__(self):
        g, t = lax.axis_index("grp"), lax.axis_index("tp")
        self.g, self.t = g, t
        self.core = g % 2
        self.z = (g // 2) % 4
        self.yh = g // 8
        self.yl = t // 4
        self.x = t % 4
        self.y = self.yh * 2 + self.yl
        self.zm = (self.z + 3) % 4
        self.zp = (self.z + 1) % 4
        self.z2 = (self.z + 2) % 4

    def at(self, y=None, z=None, x=None, core=None):
        y = self.y if y is None else y
        z = self.z if z is None else z
        x = self.x if x is None else x
        core = self.core if core is None else core
        return ((y // 2) * 4 + z) * 2 + core, (y % 2) * 4 + x


def greet(me):
    barrier = pltpu.get_barrier_semaphore()

    def signal(who):
        pl.semaphore_signal(barrier, inc=1, device_id=who, device_id_type=MESH)

    def plane(k, _):
        signal(me.at(y=(me.y + k // 4) % 4, x=(me.x + k) % 4))
        return 0

    lax.fori_loop(1, 16, plane, 0)
    signal(me.at(z=me.zp))
    signal(me.at(z=me.zm))
    for k in range(4):
        signal(me.at(y=(me.y + k) % 4, core=1 - me.core))
    for k in range(1, 4):
        signal(me.at(x=(me.x + k) % 4, core=1 - me.core))
    pl.semaphore_wait(barrier, 24)


def remote(src, dst, sent, got, who):
    return pltpu.make_async_remote_copy(
        src, dst, sent, got, device_id=who, device_id_type=MESH
    )


class Ring:
    def __init__(self, me, count, order, slot, up, down, got):
        self.me, self.count, self.order, self.slot = me, count, order, slot
        self.up, self.down, self.got = up, down, got

    def send_up(self, z, p, k):
        return remote(
            self.slot(z, p), self.slot(z, p), self.up.at[k], self.got.at[z, p],
            self.me.at(z=self.me.zp),
        )

    def send_down(self, z, p, k):
        return remote(
            self.slot(z, p), self.slot(z, p), self.down.at[k], self.got.at[z, p],
            self.me.at(z=self.me.zm),
        )

    def arrived(self, z, p):
        self.send_up(z, p, 0).wait_recv()

    def send(self, k):
        p = self.order(k)
        self.send_up(self.me.z, p, k).start()
        self.send_down(self.me.z, p, k).start()

    def pass_local(self, local):
        for k, copy in enumerate(local):
            copy.wait()
            self.send(k)

    def pass_own(self, low):
        def one(k, _):
            self.arrived(self.me.z, self.order(k))
            self.send(k)
            return 0

        lax.fori_loop(low, self.count, one, 0)

    def pass_on(self, low, high):
        me = self.me

        def two(n, _):
            p, q = self.order(2 * n), self.order(2 * n + 1)
            self.arrived(me.zm, p)
            self.send_up(me.zm, p, self.count + n).start()
            self.arrived(me.zp, p)
            self.arrived(me.zp, q)
            self.send_down(me.zp, q, self.count + n).start()
            self.arrived(me.zm, q)
            return 0

        lax.fori_loop(low, high, two, 0)

    def last(self):
        def one(k, _):
            self.arrived(self.me.z2, self.order(k))
            return 0

        lax.fori_loop(0, self.count, one, 0)

    def finish(self):
        def one(k, _):
            p = k % self.count
            self.send_up(self.me.z, p, k).wait_send()
            self.send_down(self.me.z, p, k).wait_send()
            return 0

        lax.fori_loop(0, self.count + self.count // 2, one, 0)


def ring_sems(count):
    dma = pltpu.SemaphoreType.DMA
    more = count + count // 2
    return [dma((count,)), dma((more,)), dma((more,)), dma((4, count))]


def layer_kernel(
    row_pages, last_fill, order, tok, w_qkv, w_out, cache_hbm, out,
    xbuf, qbuf, obuf, acc, squares, half_sent, half_got, full_sent, full_got,
    sq_half, sq_sum, sq_full,
    cache, pf, of_page, of_row, valid, q_pg, m_all, l_all, o_pg, joined,
    mine, ctx, o_acc, keep, give, taken, sums, final,
    own_sem, cache_sem,
    q_sent, q_up, q_down, q_got,
    w_sent, w_up, w_down, w_got,
    x_sent, x_up, x_down, x_got,
    sq_s, sq_g, h_s, h_g, f_s, f_g,
    c_up, c_down, c_core, c_got,
    y_s, y_g, e_s, e_g,
):
    me = Place()
    c = me.core
    other = me.at(core=1 - c)
    right, left = me.at(x=(me.x + 1) % 4), me.at(x=(me.x + 3) % 4)
    xl, xr, x2 = (me.x + 3) % 4, (me.x + 1) % 4, (me.x + 2) % 4
    far = me.at(y=(me.y + 2) % 4)
    near = me.at(y=me.yh * 2 + 1 - me.yl)
    greet(me)

    piece = me.yh * 2 + c

    def half(h):
        return tok.at[:, pl.ds(pl.multiple_of(h * 512, 512), 512)]

    def x_first(n):
        h = (c + n % 2) % 2
        who = me.at(y=me.yl * 2 + (me.yl + n // 2) % 2, core=h)
        return remote(half(h), xbuf.at[me.x, piece], x_sent.at[n], x_got.at[me.x, piece], who)

    stays = me.yh == me.yl

    x_here = pltpu.make_async_copy(half(c), xbuf.at[me.x, piece], own_sem.at[0])

    @pl.when(stays)
    def _():
        x_here.start()

    @pl.when(jnp.logical_not(stays))
    def _():
        x_first(0).start()

    for n in range(1, 4):
        x_first(n).start()

    def q_columns(t):
        return w_qkv.at[:, pl.ds(pl.multiple_of(t * QC, QC), QC)]

    def q_plane(k):
        t = (me.t + k) % TP
        return remote(q_columns(t), qbuf.at[me.z, me.t], q_sent.at[k], q_got.at[me.z, me.t], (me.g, t))

    def q_start(k, _):
        q_plane(k).start()
        return 0

    q_here = [pltpu.make_async_copy(q_columns(me.t), qbuf.at[me.z, me.t], own_sem.at[1])]
    q_here[0].start()
    lax.fori_loop(1, TP, q_start, 0)
    q_ring = Ring(
        me, TP, lambda k: (me.t + TP - k) % TP, lambda z, p: qbuf.at[z, p], q_up, q_down, q_got
    )

    q_ring.pass_local(q_here)

    def cached(n):
        rows = pl.ds(n * 16, 16)
        return pltpu.make_async_copy(cache_hbm.at[rows], cache.at[rows], cache_sem.at[n])

    for n in range(8):
        cached(n).start()

    def x_along(x, p, who, sem):
        return remote(xbuf.at[x, p], xbuf.at[x, p], sem, x_got.at[x, p], who)

    for n in range(4):
        p = (piece + n) % 4
        if n:
            x_along(me.x, p, right, x_up.at[0]).wait_recv()
        else:

            @pl.when(stays)
            def _():
                x_here.wait()

            @pl.when(jnp.logical_not(stays))
            def _():
                x_along(me.x, piece, right, x_up.at[0]).wait_recv()

        x_along(me.x, p, right, x_up.at[n]).start()
        x_along(me.x, p, left, x_down.at[n]).start()

    def w_columns(yl, n):
        return w_out.at[:, pl.ds(pl.multiple_of((yl * 4 + n) * OC, OC), OC)]

    def w_slot(z, p):
        return obuf.at[z, p // 4, p % 4]

    def w_plane(k):
        y, n = (me.y + k // 4) % 4, k % 4
        p = me.y * 4 + n
        return remote(w_columns(y % 2, n), w_slot(me.z, p), w_sent.at[k], w_got.at[me.z, p], me.at(y=y))

    def w_start(k, _):
        w_plane(k).start()
        return 0

    w_here = [
        pltpu.make_async_copy(w_columns(me.yl, n), w_slot(me.z, me.y * 4 + n), own_sem.at[2 + n])
        for n in range(4)
    ]
    for copy in w_here:
        copy.start()
    lax.fori_loop(4, 16, w_start, 0)
    w_ring = Ring(
        me, 16, lambda k: ((me.y + 4 - k // 4) % 4) * 4 + k % 4, w_slot, w_up, w_down, w_got
    )


    def square(x, fresh=False):
        def part(n, _):
            p, at = n // 4, pl.ds(pl.multiple_of((n % 4) * 64, 64), 64)
            v = xbuf[x, p, at, :].astype(jnp.float32)
            v = v * v
            v = v[:, :128] + v[:, 128:256] + v[:, 256:384] + v[:, 384:]
            squares[p, at, :] = v if fresh else squares[p, at, :] + v
            return 0

        lax.fori_loop(0, 16, part, 0)

    square(me.x, True)
    page_maps(row_pages, last_fill, order, of_page, of_row, valid)
    q_ring.pass_own(1)
    for n in range(4):
        x_along(xl, n, right, x_up.at[0]).wait_recv()
        x_along(xr, n, right, x_up.at[0]).wait_recv()
        if n < 2:
            x_along(xl, n, right, x_up.at[4 + n]).start()
        else:
            x_along(xr, n, left, x_down.at[2 + n]).start()
    q_ring.pass_on(0, 4)
    w_ring.pass_local(w_here)
    w_ring.pass_own(4)

    def product(z, n):
        cols = pl.ds(pl.multiple_of(n * 256, 256), 256)
        xs = xbuf[z].reshape(4 * TOK, 512)
        ws = qbuf[z, :, :, cols].reshape(512, 256)
        return cols, jnp.dot(xs, ws, preferred_element_type=jnp.float32)

    def multiply(z, fresh=False):
        def tile(n, _):
            cols, value = product(z, n)
            acc[:, cols] = value if fresh else acc[:, cols] + value
            return 0

        lax.fori_loop(0, QC // 256, tile, 0)

    gap = (me.z2 + 4 - x2) % 4
    one = (x2 + jnp.where(gap == 1, 2, 1)) % 4
    two = (x2 + jnp.where((gap == 0) | (gap == 3), 2, 3)) % 4
    three = jnp.where(gap == 0, (x2 + 3) % 4, x2)
    four = me.z2
    multiply(one, True)
    square(xl)
    square(xr)
    multiply(two)
    for n in range(4):
        x_along(x2, n, right, x_up.at[0]).wait_recv()
    square(x2)
    sq_swap = [
        remote(squares.at[2 * n + 1 - c], sq_half.at[n], sq_s.at[n], sq_g.at[n], other)
        for n in range(2)
    ]
    for copy in sq_swap:
        copy.start()
    multiply(three)
    for copy in sq_swap:
        copy.wait_recv()
    for n in range(2):
        sq_sum[n] = squares[2 * n + c] + sq_half[n]
    sq_far = remote(sq_sum.at[1 - me.yh], sq_full, sq_s.at[2], sq_g.at[2], far)
    sq_far.start()
    q_ring.last()

    def half_copy(n):
        return remote(half_sent.at[n], half_got.at[n], h_s.at[n], h_g.at[n], other)

    def full_copy(n):
        return remote(full_sent.at[n], full_got.at[n], f_s.at[n], f_g.at[n], far)

    def block(p):
        return pl.ds(pl.multiple_of(p * TOK, TOK), TOK)

    def last_tile(n):
        cols, value = product(four, n)
        acc[:, cols] += value
        for m in range(2):
            half_sent[n, m] = acc[block(2 * m + 1 - c), cols].astype(jnp.bfloat16)
        half_copy(n).start()

    for n in range(QC // 256):
        last_tile(n)

    def join_half(n):
        cols = pl.ds(pl.multiple_of(n * 256, 256), 256)
        half_copy(n).wait_recv()
        theirs = acc[block(2 * (1 - me.yh) + c), cols] + half_got[n, 1 - me.yh].astype(jnp.float32)
        full_sent[n] = theirs.astype(jnp.bfloat16)
        full_copy(n).start()
        acc[block(piece), cols] += half_got[n, me.yh].astype(jnp.float32)

    for n in range(QC // 256):
        join_half(n)
    w_ring.pass_on(0, 4)
    sq_far.wait_recv()
    mean = jnp.sum(sq_sum[me.yh] + sq_full[...], axis=1, keepdims=True) * (1.0 / D)
    gain = lax.rsqrt(mean + EPS)

    def join_full(n):
        cols = pl.ds(pl.multiple_of(n * 256, 256), 256)
        full_copy(n).wait_recv()
        total = acc[block(piece), cols] + full_got[n].astype(jnp.float32)
        total = (total * gain).astype(jnp.bfloat16).astype(jnp.float32)
        pf[2 * n], pf[2 * n + 1] = total[:, :HD], total[:, HD:]

    for n in range(QC // 256):
        join_full(n)

    page_queries(pf, of_page, q_pg)
    for n in range(8):
        cached(n).wait()
    cached_tokens(cache, q_pg, valid, m_all, l_all, o_pg)
    join_pages(pf, of_row, m_all, l_all, o_pg, joined)
    for a in range(PER_GROUP):
        mine[:, pl.ds(a * HD, HD)] = joined[a].astype(jnp.bfloat16)

    def c_along(x, core, h, sem, who):
        slot = ctx.at[x, core, h]
        return remote(slot, slot, sem, c_got.at[x, core, h], who)

    def c_first(h, sem, who):
        slot = ctx.at[me.x, c, h]
        return remote(mine.at[pl.ds(h * 128, 128)], slot, sem, c_got.at[me.x, c, h], who)

    c_here = [
        pltpu.make_async_copy(
            mine.at[pl.ds(h * 128, 128)], ctx.at[me.x, c, h], own_sem.at[6 + h]
        )
        for h in range(2)
    ]
    for h in range(2):
        c_first(h, c_up.at[h], right).start()
        c_first(h, c_down.at[h], left).start()
        c_first(h, c_core.at[h], other).start()
        c_here[h].start()
    w_ring.pass_on(4, 8)
    for h in range(2):
        c_along(xl, c, h, c_up.at[0], right).wait_recv()
        if h == 0:
            c_along(xl, c, h, c_up.at[2], right).start()
        c_along(xl, c, h, c_core.at[2 + h], other).start()
        c_along(xr, c, h, c_up.at[0], right).wait_recv()
        if h == 1:
            c_along(xr, c, h, c_down.at[2], left).start()
        c_along(xr, c, h, c_core.at[4 + h], other).start()

    def from_other(x):
        for h in range(2):
            c_along(x, 1 - c, h, c_up.at[0], right).wait_recv()

    def y_copy(j):
        return remote(give.at[j], taken.at[j], y_s.at[j], y_g.at[j], near)

    def term(j, n, fresh=False):
        ws = obuf[(me.z + j) % 4, :, n].reshape(256, OC)
        xs = ctx[n].reshape(2 * TOK, OC)
        value = lax.dot_general(
            xs, ws, (((1,), (1,)), ((), ())), preferred_element_type=jnp.float32
        )
        o_acc[j] = value if fresh else o_acc[j] + value

    def terms(n, fresh=False):
        def some(m, _):
            term((m + 3) % 4, n, fresh)
            return 0

        lax.fori_loop(0, 3, some, 0)

    def hand_over(j):
        keep[j] = o_acc[j, :, pl.ds(pl.multiple_of(me.yl * 128, 128), 128)]
        theirs = o_acc[j, :, pl.ds(pl.multiple_of((1 - me.yl) * 128, 128), 128)]
        give[j] = theirs.astype(jnp.bfloat16)
        y_copy(j).start()

    for copy in c_here:
        copy.wait()
    from_other(me.x)
    terms(me.x, True)
    from_other(xl)
    terms(xl)
    from_other(xr)
    terms(xr)
    for h in range(2):
        c_along(x2, c, h, c_up.at[0], right).wait_recv()
        c_along(x2, c, h, c_core.at[6 + h], other).start()
    from_other(x2)
    for j in (0, 1, 3):
        term(j, x2)
        hand_over(j)

    def e_copy(j, z, m):
        core = (c + m) % 2
        return remote(
            sums.at[j, core], final.at[c, me.x], e_s.at[j, m], e_g.at[c, me.x], me.at(x=z, core=core)
        )

    def spread(j, z):
        y_copy(j).wait_recv()
        total = keep[j] + taken[j].astype(jnp.float32)
        sums[j] = total.astype(jnp.bfloat16).reshape(2, TOK, 128)
        e_copy(j, z, 1).start()

        @pl.when(z != me.x)
        def _():
            e_copy(j, z, 0).start()

        @pl.when(z == me.x)
        def _():
            here = pltpu.make_async_copy(sums.at[j, c], final.at[c, me.x], own_sem.at[8])
            here.start()
            here.wait()

    w_ring.last()
    term(2, 0, True)

    def rest(n, _):
        term(2, n)
        return 0

    lax.fori_loop(1, 4, rest, 0)
    hand_over(2)
    places = [(me.z + j) % 4 for j in range(4)]
    for j in (0, 1, 3, 2):
        spread(j, places[j])

    @pl.when(jnp.logical_not(stays))
    def _():
        x_first(0).wait_send()

    for n in range(1, 4):
        x_first(n).wait_send()
    for n in range(6):
        x_along(me.x, 0, right, x_up.at[n]).wait_send()
        x_along(me.x, 0, left, x_down.at[n]).wait_send()

    def q_done(k, _):
        q_plane(k).wait_send()
        return 0

    def w_done(k, _):
        w_plane(k).wait_send()
        return 0

    lax.fori_loop(1, TP, q_done, 0)
    lax.fori_loop(4, 16, w_done, 0)
    q_ring.finish()
    w_ring.finish()
    for copy in sq_swap:
        copy.wait_send()
    sq_far.wait_send()
    for n in range(QC // 256):
        half_copy(n).wait_send()
        full_copy(n).wait_send()
    for n in range(3):
        c_along(me.x, c, 0, c_up.at[n], right).wait_send()
        c_along(me.x, c, 0, c_down.at[n], left).wait_send()
    for n in range(8):
        c_along(me.x, c, 0, c_core.at[n], other).wait_send()
    for j, z in enumerate(places):
        y_copy(j).wait_send()
        e_copy(j, z, 1).wait_send()

        @pl.when(z != me.x)
        def _(j=j, z=z):
            e_copy(j, z, 0).wait_send()

    for k in range(8):
        core, x = (c + k // 4) % 2, (me.x + k) % 4
        if k:
            remote(final.at[core, x], final.at[core, x], e_s.at[0, 0], e_g.at[core, x], other).wait_recv()

    for core in range(2):
        for yl in range(2):
            out[:, pl.ds(core * 512 + yl * 256, 256)] = jnp.concatenate(
                [final[core, x, :, pl.ds(yl * 64, 64)] for x in range(4)], axis=1
            )


def layer(row_pages, last_fill, order, tokens, w_qkv, w_out, cache):
    dma = pltpu.SemaphoreType.DMA
    inside = pl.BlockSpec(memory_space=pltpu.VMEM)
    anywhere = pl.BlockSpec(memory_space=pl.ANY)
    f32, bf16 = jnp.float32, jnp.bfloat16
    tiles = QC // 256

    def vmem(dtype, *shape):
        return pltpu.VMEM(shape, dtype)

    return pl.pallas_call(
        layer_kernel,
        out_shape=jax.ShapeDtypeStruct((TOK, OC), bf16),
        in_specs=[inside] * 3 + [anywhere] * 4,
        out_specs=pl.BlockSpec(memory_space=pltpu.VMEM),
        scratch_shapes=[
            vmem(bf16, 4, 4, TOK, 512),
            vmem(bf16, 4, TP, 64, QC),
            vmem(bf16, 4, 4, 4, 64, OC),
            vmem(f32, 4 * TOK, QC),
            vmem(f32, 4, TOK, 128),
            vmem(bf16, tiles, 2, TOK, 256),
            vmem(bf16, tiles, 2, TOK, 256),
            vmem(bf16, tiles, TOK, 256),
            vmem(bf16, tiles, TOK, 256),
            vmem(f32, 2, TOK, 128),
            vmem(f32, 2, TOK, 128),
            vmem(f32, TOK, 128),
            vmem(bf16, PAGES, 2 * BLOCK, HD),
            vmem(f32, PER_GROUP + 2, TOK, HD),
            vmem(f32, PAGES, PAGES),
            vmem(f32, ROWS, PAGES),
            vmem(f32, PAGES, PAGES),
            vmem(f32, PAGES * 32, HD),
            vmem(f32, 32, PAGES),
            vmem(f32, 32, PAGES),
            vmem(f32, PAGES * 32, HD),
            vmem(f32, PER_GROUP, TOK, HD),
            vmem(bf16, TOK, OC),
            vmem(bf16, 4, 2, 2, 128, OC),
            vmem(f32, 4, 2 * TOK, 256),
            vmem(f32, 4, 2 * TOK, 128),
            vmem(bf16, 4, 2 * TOK, 128),
            vmem(bf16, 4, 2 * TOK, 128),
            vmem(bf16, 4, 2, TOK, 128),
            vmem(bf16, 2, 4, TOK, 128),
            dma((9,)),
            dma((8,)),
        ]
        + ring_sems(TP)
        + ring_sems(16)
        + [dma((4,)), dma((6,)), dma((6,)), dma((4, 4))]
        + [dma((3,)), dma((3,)), dma((tiles,)), dma((tiles,)), dma((tiles,)), dma((tiles,))]
        + [dma((3,)), dma((3,)), dma((8,)), dma((4, 2, 2))]
        + [dma((4,)), dma((4,)), dma((4, 2)), dma((2, 4))],
        compiler_params=pltpu.CompilerParams(
            collective_id=0, has_side_effects=True, vmem_limit_bytes=60 * MIB
        ),
        cost_estimate=pl.CostEstimate(
            flops=2 * TOK * D * (QC + OC), bytes_accessed=16 * MIB, transcendentals=0
        ),
        name="layer",
    )(row_pages, last_fill, order, tokens, w_qkv, w_out, cache)


def per_device(tokens, w_qkv, w_out, kv_cache, row_pages, last_fill, page_order):
    mixed = layer(
        row_pages, last_fill, page_order,
        tokens.reshape(TOK, -1), w_qkv, w_out, kv_cache.reshape(PAGES, 2 * BLOCK, HD),
    )
    return mixed.reshape(ROWS, STEPS, -1)


def solution(mesh):
    placed = (
        P("grp", None, "tp"),
        P(("grp", "tp"), None),
        P(("grp", "tp"), None),
        P("grp", None, None, "tp"),
        P("grp", None),
        P("grp", None),
        P("grp", None),
    )
    return jax.shard_map(
        per_device, mesh=mesh, in_specs=placed, out_specs=P("grp", None, "tp"), check_vma=False
    )
```

```python
import jax
import jax.numpy as jnp
from jax import lax
from jax.experimental import pallas as pl
from jax.experimental.pallas import tpu as pltpu
from jax.sharding import PartitionSpec as P

HD = 128
STEPS = 4
PER_GROUP = 8
BLOCK = 128
ROWS = 64
PAGES = 128
TOK = ROWS * STEPS
D = 8192
TP = 8
QC = 1280
OC = 1024
EPS = 1e-05
SCALE = HD ** (-0.5)
MESH = pl.DeviceIdType.MESH
MIB = 1 << 20


def page_maps(row_pages, last_fill, order, of_page, of_row, valid):
    f32 = jnp.float32
    none = jnp.zeros((1, PAGES - ROWS), f32)
    pages = jnp.concatenate([row_pages[...].astype(f32), none], axis=1)
    fill = jnp.concatenate([last_fill[...].astype(f32), none], axis=1)
    down = lax.broadcasted_iota(jnp.int32, (PAGES, PAGES), 0)
    along = lax.broadcasted_iota(jnp.int32, (PAGES, PAGES), 1)
    upto = jnp.where(down <= along, 1.0, 0.0)
    end = jnp.dot(jnp.broadcast_to(pages, (8, PAGES)), upto, preferred_element_type=f32)[0:1]
    place = jnp.sum(
        jnp.where(order[...] == down, along.astype(f32), 0.0), axis=1, keepdims=True
    )
    mine = (place >= end - pages) & (place < end)
    used = jnp.where(place == end - 1.0, fill, float(BLOCK))
    valid[...] = jnp.broadcast_to(
        jnp.sum(jnp.where(mine, used, 0.0), axis=1, keepdims=True), (PAGES, PAGES)
    )
    found = jnp.where(mine, 1.0, 0.0)
    of_page[...] = found
    of_row[...] = found.T[:ROWS]


def page_queries(pf, of_page, q_pg):
    def head(a, _):
        for step in range(STEPS):
            q = pf[a, pl.ds(step, ROWS, stride=STEPS), :]
            q_pg[pl.ds(a * STEPS + step, PAGES, stride=32), :] = jnp.dot(
                of_page[:, :ROWS], q, preferred_element_type=jnp.float32
            )
        return 0

    lax.fori_loop(0, PER_GROUP, head, 0)


def cached_tokens(cache, q_pg, valid, m_all, l_all, o_pg):
    n_at = 16
    lane = lax.broadcasted_iota(jnp.int32, (1, 2 * BLOCK), 1)
    lane = jnp.where((lane & 1) == 0, lane.astype(jnp.float32), 1e6)
    page = lax.broadcasted_iota(jnp.int32, (32, PAGES), 1)

    def some(n, run):
        m_run, l_run = run
        slots = [n * n_at + k for k in range(n_at)]
        pages = [cache[i] for i in slots]
        rows = [pl.ds(pl.multiple_of(i * 32, 32), 32) for i in slots]
        raw = [
            lax.dot_general(
                q_pg[at, :].astype(jnp.bfloat16), kv, (((1,), (1,)), ((), ())),
                preferred_element_type=jnp.float32,
            )
            for at, kv in zip(rows, pages)
        ]
        ends = [valid[pl.ds(i, 1), :] * 2.0 for i in slots]
        ends = [jnp.concatenate([e, e], axis=1) for e in ends]
        raw = [s * SCALE + jnp.where(lane < e, 0.0, -jnp.inf) for s, e in zip(raw, ends)]
        tops = [jnp.max(s, axis=1, keepdims=True) for s in raw]
        probs = [jnp.exp(s - m) for s, m in zip(raw, tops)]
        totals = [jnp.sum(p, axis=1, keepdims=True) for p in probs]
        moved = [pltpu.roll(p, 1, 1).astype(jnp.bfloat16) for p in probs]
        outs = [
            jnp.dot(w, kv, preferred_element_type=jnp.float32)
            for w, kv in zip(moved, pages)
        ]
        for k, i in enumerate(slots):
            o_pg[rows[k], :] = outs[k]
            m_run = jnp.where(page == i, tops[k], m_run)
            l_run = jnp.where(page == i, totals[k], l_run)
        return m_run, l_run

    zero = jnp.zeros((32, PAGES), jnp.float32)
    m_all[...], l_all[...] = lax.fori_loop(0, PAGES // n_at, some, (zero, zero))


def join_pages(pf, of_row, m_all, l_all, o_pg, joined):
    def head(a, _):
        for step in range(STEPS):
            h = a * STEPS + step
            rows = pl.ds(step, ROWS, stride=STEPS)
            q = pf[a, rows, :]
            fresh = [
                jnp.sum(
                    q * pf[PER_GROUP, pl.ds(u, ROWS, stride=STEPS), :], axis=1, keepdims=True
                )
                * SCALE
                for u in range(step + 1)
            ]
            tops = jnp.where(of_row[...] > 0.5, m_all[pl.ds(h, 1), :], -jnp.inf)
            top = jnp.max(tops, axis=1, keepdims=True)
            for s in fresh:
                top = jnp.maximum(top, s)
            share = jnp.exp(tops - top)
            total = jnp.sum(share * l_all[pl.ds(h, 1), :], axis=1, keepdims=True)
            out = jnp.dot(
                share, o_pg[pl.ds(h, PAGES, stride=32), :],
                preferred_element_type=jnp.float32, precision=lax.Precision.HIGHEST,
            )
            for u, s in enumerate(fresh):
                p = jnp.exp(s - top)
                total = total + p
                out = out + p * pf[PER_GROUP + 1, pl.ds(u, ROWS, stride=STEPS), :]
            joined[a, rows, :] = out / total
        return 0

    lax.fori_loop(0, PER_GROUP, head, 0)


class Place:
    def __init__(self):
        g, t = lax.axis_index("grp"), lax.axis_index("tp")
        self.g, self.t = g, t
        self.core = g % 2
        self.z = (g // 2) % 4
        self.yh = g // 8
        self.yl = t // 4
        self.x = t % 4
        self.y = self.yh * 2 + self.yl
        self.zm = (self.z + 3) % 4
        self.zp = (self.z + 1) % 4
        self.z2 = (self.z + 2) % 4

    def at(self, y=None, z=None, x=None, core=None):
        y = self.y if y is None else y
        z = self.z if z is None else z
        x = self.x if x is None else x
        core = self.core if core is None else core
        return ((y // 2) * 4 + z) * 2 + core, (y % 2) * 4 + x


def greet(me):
    barrier = pltpu.get_barrier_semaphore()

    def signal(who):
        pl.semaphore_signal(barrier, inc=1, device_id=who, device_id_type=MESH)

    def plane(k, _):
        signal(me.at(y=(me.y + k // 4) % 4, x=(me.x + k) % 4))
        return 0

    lax.fori_loop(1, 16, plane, 0)
    signal(me.at(z=me.zp))
    signal(me.at(z=me.zm))
    for k in range(4):
        signal(me.at(y=(me.y + k) % 4, core=1 - me.core))
    for k in range(1, 4):
        signal(me.at(x=(me.x + k) % 4, core=1 - me.core))
    pl.semaphore_wait(barrier, 24)


def remote(src, dst, sent, got, who):
    return pltpu.make_async_remote_copy(
        src, dst, sent, got, device_id=who, device_id_type=MESH
    )


class Ring:
    def __init__(self, me, count, order, slot, up, down, got):
        self.me, self.count, self.order, self.slot = me, count, order, slot
        self.up, self.down, self.got = up, down, got

    def send_up(self, z, p, k):
        return remote(
            self.slot(z, p), self.slot(z, p), self.up.at[k], self.got.at[z, p],
            self.me.at(z=self.me.zp),
        )

    def send_down(self, z, p, k):
        return remote(
            self.slot(z, p), self.slot(z, p), self.down.at[k], self.got.at[z, p],
            self.me.at(z=self.me.zm),
        )

    def arrived(self, z, p):
        self.send_up(z, p, 0).wait_recv()

    def send(self, k):
        p = self.order(k)
        self.send_up(self.me.z, p, k).start()
        self.send_down(self.me.z, p, k).start()

    def pass_local(self, local):
        for k, copy in enumerate(local):
            copy.wait()
            self.send(k)

    def pass_own(self, low):
        def one(k, _):
            self.arrived(self.me.z, self.order(k))
            self.send(k)
            return 0

        lax.fori_loop(low, self.count, one, 0)

    def pass_on(self, low, high):
        me = self.me

        def two(n, _):
            p, q = self.order(2 * n), self.order(2 * n + 1)
            self.arrived(me.zm, p)
            self.send_up(me.zm, p, self.count + n).start()
            self.arrived(me.zp, p)
            self.arrived(me.zp, q)
            self.send_down(me.zp, q, self.count + n).start()
            self.arrived(me.zm, q)
            return 0

        lax.fori_loop(low, high, two, 0)

    def last(self, low, high):
        def one(k, _):
            self.arrived(self.me.z2, self.order(k))
            return 0

        lax.fori_loop(low, high, one, 0)

    def finish(self):
        def one(k, _):
            p = k % self.count
            self.send_up(self.me.z, p, k).wait_send()
            self.send_down(self.me.z, p, k).wait_send()
            return 0

        lax.fori_loop(0, self.count + self.count // 2, one, 0)


def ring_sems(count):
    dma = pltpu.SemaphoreType.DMA
    more = count + count // 2
    return [dma((count,)), dma((more,)), dma((more,)), dma((4, count))]


def layer_kernel(
    row_pages, last_fill, order, tok, w_qkv, w_out, cache_hbm, out,
    xbuf, qbuf, obuf, acc, squares, half_sent, half_got, full_sent, full_got,
    sq_half, sq_sum, sq_full,
    cache, pf, of_page, of_row, valid, q_pg, m_all, l_all, o_pg, joined,
    mine, ctx, o_acc, keep, give, taken, sums, final,
    own_sem, cache_sem,
    q_sent, q_up, q_down, q_got,
    w_sent, w_up, w_down, w_got, v_sent,
    x_sent, x_up, x_down, x_got,
    sq_s, sq_g, h_s, h_g, f_s, f_g,
    c_up, c_down, c_core, c_got,
    y_s, y_g, e_s, e_g,
):
    me = Place()
    c = me.core
    other = me.at(core=1 - c)
    right, left = me.at(x=(me.x + 1) % 4), me.at(x=(me.x + 3) % 4)
    xl, xr, x2 = (me.x + 3) % 4, (me.x + 1) % 4, (me.x + 2) % 4
    far = me.at(y=(me.y + 2) % 4)
    near = me.at(y=me.yh * 2 + 1 - me.yl)
    greet(me)

    piece = me.yh * 2 + c

    def half(h):
        return tok.at[:, pl.ds(pl.multiple_of(h * 512, 512), 512)]

    def x_first(n):
        h = (c + n % 2) % 2
        who = me.at(y=me.yl * 2 + (me.yl + n // 2) % 2, core=h)
        return remote(half(h), xbuf.at[me.x, piece], x_sent.at[n], x_got.at[me.x, piece], who)

    stays = me.yh == me.yl

    x_here = pltpu.make_async_copy(half(c), xbuf.at[me.x, piece], own_sem.at[0])

    @pl.when(stays)
    def _():
        x_here.start()

    @pl.when(jnp.logical_not(stays))
    def _():
        x_first(0).start()

    for n in range(1, 4):
        x_first(n).start()

    def q_columns(t):
        return w_qkv.at[:, pl.ds(pl.multiple_of(t * QC, QC), QC)]

    def q_plane(k):
        t = (me.t + k) % TP
        return remote(q_columns(t), qbuf.at[me.z, me.t], q_sent.at[k], q_got.at[me.z, me.t], (me.g, t))

    def q_start(k, _):
        q_plane(k).start()
        return 0

    q_here = [pltpu.make_async_copy(q_columns(me.t), qbuf.at[me.z, me.t], own_sem.at[1])]
    q_here[0].start()
    lax.fori_loop(1, TP, q_start, 0)
    q_ring = Ring(
        me, TP, lambda k: (me.t + TP - k) % TP, lambda z, p: qbuf.at[z, p], q_up, q_down, q_got
    )

    q_ring.pass_local(q_here)

    def cached(n):
        rows = pl.ds(n * 16, 16)
        return pltpu.make_async_copy(cache_hbm.at[rows], cache.at[rows], cache_sem.at[n])

    for n in range(8):
        cached(n).start()

    def x_along(x, p, who, sem):
        return remote(xbuf.at[x, p], xbuf.at[x, p], sem, x_got.at[x, p], who)

    for n in range(4):
        p = (piece + n) % 4
        if n:
            x_along(me.x, p, right, x_up.at[0]).wait_recv()
        else:

            @pl.when(stays)
            def _():
                x_here.wait()

            @pl.when(jnp.logical_not(stays))
            def _():
                x_along(me.x, piece, right, x_up.at[0]).wait_recv()

        x_along(me.x, p, right, x_up.at[n]).start()
        x_along(me.x, p, left, x_down.at[n]).start()

    def w_columns(yl, n):
        return w_out.at[:, pl.ds(pl.multiple_of((yl * 4 + n) * OC, OC), OC)]

    def w_slot(z, p):
        return obuf.at[z, p // 4, p % 4]

    def w_plane(k):
        y = jnp.where(k == 4, me.yh * 2 + 1 - me.yl, (me.y + 1 + (k - 5) // 3) % 4)
        n = jnp.where(k == 4, 3, (k - 5) % 3)
        p = me.y * 4 + n
        return remote(w_columns(y % 2, n), w_slot(me.z, p), w_sent.at[k], w_got.at[me.z, p], me.at(y=y))

    def w_order(k):
        first = me.y * 4 + (k + 3) % 4
        later = ((me.y + 3 - (k - 5) // 3) % 4) * 4 + (k - 5) % 3
        swap = (me.yh * 2 + 1 - me.yl) * 4 + 3
        return jnp.where(k < 4, first, jnp.where(k == 4, swap, later))

    def w_far(j, m):
        z, p = (me.z + j) % 4, (me.yh * 2 + m) * 4 + 3
        return remote(w_slot(z, p), w_slot(z, p), v_sent.at[j, m], w_got.at[z, p], far)

    def w_cross(j):
        for m in range(2):
            w_far(j, m).start()

    def w_crossed(j):
        for m in range(2):
            w_ring.arrived((me.z + j) % 4, ((1 - me.yh) * 2 + m) * 4 + 3)

    def w_start(k, _):
        w_plane(k).start()
        return 0

    w_here = [
        pltpu.make_async_copy(w_columns(me.yl, n), w_slot(me.z, me.y * 4 + n), own_sem.at[2 + n])
        for n in (3, 0, 1, 2)
    ]
    for copy in w_here:
        copy.start()
    lax.fori_loop(4, 14, w_start, 0)
    w_ring = Ring(
        me, 14, w_order, w_slot, w_up, w_down, w_got
    )


    def square(x, fresh=False):
        def part(n, _):
            p, at = n // 4, pl.ds(pl.multiple_of((n % 4) * 64, 64), 64)
            v = xbuf[x, p, at, :].astype(jnp.float32)
            v = v * v
            v = v[:, :128] + v[:, 128:256] + v[:, 256:384] + v[:, 384:]
            squares[p, at, :] = v if fresh else squares[p, at, :] + v
            return 0

        lax.fori_loop(0, 16, part, 0)

    square(me.x, True)
    page_maps(row_pages, last_fill, order, of_page, of_row, valid)
    q_ring.pass_own(1)
    for n in range(4):
        x_along(xl, n, right, x_up.at[0]).wait_recv()
        x_along(xr, n, right, x_up.at[0]).wait_recv()
        if n < 2:
            x_along(xl, n, right, x_up.at[4 + n]).start()
        else:
            x_along(xr, n, left, x_down.at[2 + n]).start()
    q_ring.pass_on(0, 4)
    w_ring.pass_local(w_here)
    w_ring.pass_own(4)
    w_cross(0)

    def product(z, n):
        cols = pl.ds(pl.multiple_of(n * 256, 256), 256)
        xs = xbuf[z].reshape(4 * TOK, 512)
        ws = qbuf[z, :, :, cols].reshape(512, 256)
        return cols, jnp.dot(xs, ws, preferred_element_type=jnp.float32)

    def multiply(z, fresh=False):
        def tile(n, _):
            cols, value = product(z, n)
            acc[:, cols] = value if fresh else acc[:, cols] + value
            return 0

        lax.fori_loop(0, QC // 256, tile, 0)

    gap = (me.z2 + 4 - x2) % 4
    one = (x2 + jnp.where(gap == 1, 2, 1)) % 4
    two = (x2 + jnp.where((gap == 0) | (gap == 3), 2, 3)) % 4
    three = jnp.where(gap == 0, (x2 + 3) % 4, x2)
    four = me.z2
    multiply(one, True)
    square(xl)
    square(xr)
    multiply(two)
    for n in range(4):
        x_along(x2, n, right, x_up.at[0]).wait_recv()
    square(x2)
    sq_swap = [
        remote(squares.at[2 * n + 1 - c], sq_half.at[n], sq_s.at[n], sq_g.at[n], other)
        for n in range(2)
    ]
    for copy in sq_swap:
        copy.start()
    multiply(three)
    for copy in sq_swap:
        copy.wait_recv()
    for n in range(2):
        sq_sum[n] = squares[2 * n + c] + sq_half[n]
    sq_far = remote(sq_sum.at[1 - me.yh], sq_full, sq_s.at[2], sq_g.at[2], far)
    sq_far.start()
    q_ring.last(0, TP)

    def half_copy(n):
        return remote(half_sent.at[n], half_got.at[n], h_s.at[n], h_g.at[n], other)

    def full_copy(n):
        return remote(full_sent.at[n], full_got.at[n], f_s.at[n], f_g.at[n], far)

    def block(p):
        return pl.ds(pl.multiple_of(p * TOK, TOK), TOK)

    def last_tile(n):
        cols, value = product(four, n)
        acc[:, cols] += value
        for m in range(2):
            half_sent[n, m] = acc[block(2 * m + 1 - c), cols].astype(jnp.bfloat16)
        half_copy(n).start()

    for n in range(QC // 256):
        last_tile(n)

    def join_half(n):
        cols = pl.ds(pl.multiple_of(n * 256, 256), 256)
        half_copy(n).wait_recv()
        theirs = acc[block(2 * (1 - me.yh) + c), cols] + half_got[n, 1 - me.yh].astype(jnp.float32)
        full_sent[n] = theirs.astype(jnp.bfloat16)
        full_copy(n).start()
        acc[block(piece), cols] += half_got[n, me.yh].astype(jnp.float32)

    for n in range(QC // 256):
        join_half(n)
    w_ring.pass_on(0, 4)
    w_cross(1)
    w_cross(3)
    sq_far.wait_recv()
    mean = jnp.sum(sq_sum[me.yh] + sq_full[...], axis=1, keepdims=True) * (1.0 / D)
    gain = lax.rsqrt(mean + EPS)

    def join_full(n):
        cols = pl.ds(pl.multiple_of(n * 256, 256), 256)
        full_copy(n).wait_recv()
        total = acc[block(piece), cols] + full_got[n].astype(jnp.float32)
        total = (total * gain).astype(jnp.bfloat16).astype(jnp.float32)
        pf[2 * n], pf[2 * n + 1] = total[:, :HD], total[:, HD:]

    for n in range(QC // 256):
        join_full(n)

    page_queries(pf, of_page, q_pg)
    for n in range(8):
        cached(n).wait()
    cached_tokens(cache, q_pg, valid, m_all, l_all, o_pg)
    join_pages(pf, of_row, m_all, l_all, o_pg, joined)
    for a in range(PER_GROUP):
        mine[:, pl.ds(a * HD, HD)] = joined[a].astype(jnp.bfloat16)

    def c_along(x, core, h, sem, who):
        slot = ctx.at[x, core, h]
        return remote(slot, slot, sem, c_got.at[x, core, h], who)

    def c_first(h, sem, who):
        slot = ctx.at[me.x, c, h]
        return remote(mine.at[pl.ds(h * 128, 128)], slot, sem, c_got.at[me.x, c, h], who)

    c_here = [
        pltpu.make_async_copy(
            mine.at[pl.ds(h * 128, 128)], ctx.at[me.x, c, h], own_sem.at[6 + h]
        )
        for h in range(2)
    ]
    for h in range(2):
        c_first(h, c_up.at[h], right).start()
        c_first(h, c_down.at[h], left).start()
        c_first(h, c_core.at[h], other).start()
        c_here[h].start()
    w_ring.pass_on(4, 7)
    w_ring.arrived(me.z2, w_order(0))
    w_ring.arrived(me.z2, w_order(4))
    w_cross(2)
    for h in range(2):
        c_along(xl, c, h, c_up.at[0], right).wait_recv()
        if h == 0:
            c_along(xl, c, h, c_up.at[2], right).start()
        c_along(xl, c, h, c_core.at[2 + h], other).start()
        c_along(xr, c, h, c_up.at[0], right).wait_recv()
        if h == 1:
            c_along(xr, c, h, c_down.at[2], left).start()
        c_along(xr, c, h, c_core.at[4 + h], other).start()

    def from_other(x):
        for h in range(2):
            c_along(x, 1 - c, h, c_up.at[0], right).wait_recv()

    def y_copy(j):
        return remote(give.at[j], taken.at[j], y_s.at[j], y_g.at[j], near)

    def term(j, n, fresh=False):
        ws = obuf[(me.z + j) % 4, :, n].reshape(256, OC)
        xs = ctx[n].reshape(2 * TOK, OC)
        value = lax.dot_general(
            xs, ws, (((1,), (1,)), ((), ())), preferred_element_type=jnp.float32
        )
        o_acc[j] = value if fresh else o_acc[j] + value

    def terms(n, fresh=False):
        def some(m, _):
            term((m + 3) % 4, n, fresh)
            return 0

        lax.fori_loop(0, 3, some, 0)

    def hand_over(j):
        keep[j] = o_acc[j, :, pl.ds(pl.multiple_of(me.yl * 128, 128), 128)]
        theirs = o_acc[j, :, pl.ds(pl.multiple_of((1 - me.yl) * 128, 128), 128)]
        give[j] = theirs.astype(jnp.bfloat16)
        y_copy(j).start()

    for copy in c_here:
        copy.wait()
    from_other(me.x)
    for j in (0, 1, 3):
        w_crossed(j)
    terms(me.x, True)
    from_other(xl)
    terms(xl)
    from_other(xr)
    terms(xr)
    for h in range(2):
        c_along(x2, c, h, c_up.at[0], right).wait_recv()
        c_along(x2, c, h, c_core.at[6 + h], other).start()
    from_other(x2)
    for j in (0, 1, 3):
        term(j, x2)
        hand_over(j)

    def e_copy(j, z, m):
        core = (c + m) % 2
        return remote(
            sums.at[j, core], final.at[c, me.x], e_s.at[j, m], e_g.at[c, me.x], me.at(x=z, core=core)
        )

    def spread(j, z):
        y_copy(j).wait_recv()
        total = keep[j] + taken[j].astype(jnp.float32)
        sums[j] = total.astype(jnp.bfloat16).reshape(2, TOK, 128)
        e_copy(j, z, 1).start()

        @pl.when(z != me.x)
        def _():
            e_copy(j, z, 0).start()

        @pl.when(z == me.x)
        def _():
            here = pltpu.make_async_copy(sums.at[j, c], final.at[c, me.x], own_sem.at[8])
            here.start()
            here.wait()

    w_ring.last(1, 4)
    w_ring.last(5, 14)
    w_crossed(2)
    term(2, 0, True)

    def rest(n, _):
        term(2, n)
        return 0

    lax.fori_loop(1, 4, rest, 0)
    hand_over(2)
    places = [(me.z + j) % 4 for j in range(4)]
    for j in (0, 1, 3, 2):
        spread(j, places[j])

    @pl.when(jnp.logical_not(stays))
    def _():
        x_first(0).wait_send()

    for n in range(1, 4):
        x_first(n).wait_send()
    for n in range(6):
        x_along(me.x, 0, right, x_up.at[n]).wait_send()
        x_along(me.x, 0, left, x_down.at[n]).wait_send()

    def q_done(k, _):
        q_plane(k).wait_send()
        return 0

    def w_done(k, _):
        w_plane(k).wait_send()
        return 0

    lax.fori_loop(1, TP, q_done, 0)
    lax.fori_loop(4, 14, w_done, 0)
    for j in range(4):
        for m in range(2):
            w_far(j, m).wait_send()
    q_ring.finish()
    w_ring.finish()
    for copy in sq_swap:
        copy.wait_send()
    sq_far.wait_send()
    for n in range(QC // 256):
        half_copy(n).wait_send()
        full_copy(n).wait_send()
    for n in range(3):
        c_along(me.x, c, 0, c_up.at[n], right).wait_send()
        c_along(me.x, c, 0, c_down.at[n], left).wait_send()
    for n in range(8):
        c_along(me.x, c, 0, c_core.at[n], other).wait_send()
    for j, z in enumerate(places):
        y_copy(j).wait_send()
        e_copy(j, z, 1).wait_send()

        @pl.when(z != me.x)
        def _(j=j, z=z):
            e_copy(j, z, 0).wait_send()

    for k in range(8):
        core, x = (c + k // 4) % 2, (me.x + k) % 4
        if k:
            remote(final.at[core, x], final.at[core, x], e_s.at[0, 0], e_g.at[core, x], other).wait_recv()

    for core in range(2):
        for yl in range(2):
            out[:, pl.ds(core * 512 + yl * 256, 256)] = jnp.concatenate(
                [final[core, x, :, pl.ds(yl * 64, 64)] for x in range(4)], axis=1
            )


def layer(row_pages, last_fill, order, tokens, w_qkv, w_out, cache):
    dma = pltpu.SemaphoreType.DMA
    inside = pl.BlockSpec(memory_space=pltpu.VMEM)
    anywhere = pl.BlockSpec(memory_space=pl.ANY)
    f32, bf16 = jnp.float32, jnp.bfloat16
    tiles = QC // 256

    def vmem(dtype, *shape):
        return pltpu.VMEM(shape, dtype)

    return pl.pallas_call(
        layer_kernel,
        out_shape=jax.ShapeDtypeStruct((TOK, OC), bf16),
        in_specs=[inside] * 3 + [anywhere] * 4,
        out_specs=pl.BlockSpec(memory_space=pltpu.VMEM),
        scratch_shapes=[
            vmem(bf16, 4, 4, TOK, 512),
            vmem(bf16, 4, TP, 64, QC),
            vmem(bf16, 4, 4, 4, 64, OC),
            vmem(f32, 4 * TOK, QC),
            vmem(f32, 4, TOK, 128),
            vmem(bf16, tiles, 2, TOK, 256),
            vmem(bf16, tiles, 2, TOK, 256),
            vmem(bf16, tiles, TOK, 256),
            vmem(bf16, tiles, TOK, 256),
            vmem(f32, 2, TOK, 128),
            vmem(f32, 2, TOK, 128),
            vmem(f32, TOK, 128),
            vmem(bf16, PAGES, 2 * BLOCK, HD),
            vmem(f32, PER_GROUP + 2, TOK, HD),
            vmem(f32, PAGES, PAGES),
            vmem(f32, ROWS, PAGES),
            vmem(f32, PAGES, PAGES),
            vmem(f32, PAGES * 32, HD),
            vmem(f32, 32, PAGES),
            vmem(f32, 32, PAGES),
            vmem(f32, PAGES * 32, HD),
            vmem(f32, PER_GROUP, TOK, HD),
            vmem(bf16, TOK, OC),
            vmem(bf16, 4, 2, 2, 128, OC),
            vmem(f32, 4, 2 * TOK, 256),
            vmem(f32, 4, 2 * TOK, 128),
            vmem(bf16, 4, 2 * TOK, 128),
            vmem(bf16, 4, 2 * TOK, 128),
            vmem(bf16, 4, 2, TOK, 128),
            vmem(bf16, 2, 4, TOK, 128),
            dma((9,)),
            dma((8,)),
        ]
        + ring_sems(TP)
        + [dma((14,)), dma((21,)), dma((21,)), dma((4, 16)), dma((4, 2))]
        + [dma((4,)), dma((6,)), dma((6,)), dma((4, 4))]
        + [dma((3,)), dma((3,)), dma((tiles,)), dma((tiles,)), dma((tiles,)), dma((tiles,))]
        + [dma((3,)), dma((3,)), dma((8,)), dma((4, 2, 2))]
        + [dma((4,)), dma((4,)), dma((4, 2)), dma((2, 4))],
        compiler_params=pltpu.CompilerParams(
            collective_id=0, has_side_effects=True, vmem_limit_bytes=60 * MIB
        ),
        cost_estimate=pl.CostEstimate(
            flops=2 * TOK * D * (QC + OC), bytes_accessed=16 * MIB, transcendentals=0
        ),
        name="layer",
    )(row_pages, last_fill, order, tokens, w_qkv, w_out, cache)


def per_device(tokens, w_qkv, w_out, kv_cache, row_pages, last_fill, page_order):
    mixed = layer(
        row_pages, last_fill, page_order,
        tokens.reshape(TOK, -1), w_qkv, w_out, kv_cache.reshape(PAGES, 2 * BLOCK, HD),
    )
    return mixed.reshape(ROWS, STEPS, -1)


def solution(mesh):
    placed = (
        P("grp", None, "tp"),
        P(("grp", "tp"), None),
        P(("grp", "tp"), None),
        P("grp", None, None, "tp"),
        P("grp", None),
        P("grp", None),
        P("grp", None),
    )
    return jax.shard_map(
        per_device, mesh=mesh, in_specs=placed, out_specs=P("grp", None, "tp"), check_vma=False
    )
```

```python
import jax
import jax.numpy as jnp
from jax import lax
from jax.experimental import pallas as pl
from jax.experimental.pallas import tpu as pltpu
from jax.sharding import PartitionSpec as P

HD = 128
STEPS = 4
PER_GROUP = 8
BLOCK = 128
ROWS = 64
PAGES = 128
TOK = ROWS * STEPS
D = 8192
TP = 8
QC = 1280
OC = 1024
EPS = 1e-05
SCALE = HD ** (-0.5)
MESH = pl.DeviceIdType.MESH
MIB = 1 << 20


def page_maps(row_pages, last_fill, order, of_page, of_row, valid):
    f32 = jnp.float32
    none = jnp.zeros((1, PAGES - ROWS), f32)
    pages = jnp.concatenate([row_pages[...].astype(f32), none], axis=1)
    fill = jnp.concatenate([last_fill[...].astype(f32), none], axis=1)
    down = lax.broadcasted_iota(jnp.int32, (PAGES, PAGES), 0)
    along = lax.broadcasted_iota(jnp.int32, (PAGES, PAGES), 1)
    upto = jnp.where(down <= along, 1.0, 0.0)
    end = jnp.dot(jnp.broadcast_to(pages, (8, PAGES)), upto, preferred_element_type=f32)[0:1]
    place = jnp.sum(
        jnp.where(order[...] == down, along.astype(f32), 0.0), axis=1, keepdims=True
    )
    mine = (place >= end - pages) & (place < end)
    used = jnp.where(place == end - 1.0, fill, float(BLOCK))
    valid[...] = jnp.broadcast_to(
        jnp.sum(jnp.where(mine, used, 0.0), axis=1, keepdims=True), (PAGES, PAGES)
    )
    found = jnp.where(mine, 1.0, 0.0)
    of_page[...] = found
    of_row[...] = found.T[:ROWS]


def page_queries(pf, of_page, q_pg):
    def head(a, _):
        for step in range(STEPS):
            q = pf[a, pl.ds(step, ROWS, stride=STEPS), :]
            q_pg[pl.ds(a * STEPS + step, PAGES, stride=32), :] = jnp.dot(
                of_page[:, :ROWS], q, preferred_element_type=jnp.float32
            )
        return 0

    lax.fori_loop(0, PER_GROUP, head, 0)


def cached_tokens(cache, q_pg, valid, m_all, l_all, o_pg):
    n_at = 16
    lane = lax.broadcasted_iota(jnp.int32, (1, 2 * BLOCK), 1)
    lane = jnp.where((lane & 1) == 0, lane.astype(jnp.float32), 1e6)
    page = lax.broadcasted_iota(jnp.int32, (32, PAGES), 1)

    def some(n, run):
        m_run, l_run = run
        slots = [n * n_at + k for k in range(n_at)]
        pages = [cache[i] for i in slots]
        rows = [pl.ds(pl.multiple_of(i * 32, 32), 32) for i in slots]
        raw = [
            lax.dot_general(
                q_pg[at, :].astype(jnp.bfloat16), kv, (((1,), (1,)), ((), ())),
                preferred_element_type=jnp.float32,
            )
            for at, kv in zip(rows, pages)
        ]
        ends = [valid[pl.ds(i, 1), :] * 2.0 for i in slots]
        ends = [jnp.concatenate([e, e], axis=1) for e in ends]
        raw = [s * SCALE + jnp.where(lane < e, 0.0, -jnp.inf) for s, e in zip(raw, ends)]
        tops = [jnp.max(s, axis=1, keepdims=True) for s in raw]
        probs = [jnp.exp(s - m) for s, m in zip(raw, tops)]
        totals = [jnp.sum(p, axis=1, keepdims=True) for p in probs]
        moved = [pltpu.roll(p, 1, 1).astype(jnp.bfloat16) for p in probs]
        outs = [
            jnp.dot(w, kv, preferred_element_type=jnp.float32)
            for w, kv in zip(moved, pages)
        ]
        for k, i in enumerate(slots):
            o_pg[rows[k], :] = outs[k]
            m_run = jnp.where(page == i, tops[k], m_run)
            l_run = jnp.where(page == i, totals[k], l_run)
        return m_run, l_run

    zero = jnp.zeros((32, PAGES), jnp.float32)
    m_all[...], l_all[...] = lax.fori_loop(0, PAGES // n_at, some, (zero, zero))


def join_pages(pf, of_row, m_all, l_all, o_pg, joined):
    def head(a, _):
        for step in range(STEPS):
            h = a * STEPS + step
            rows = pl.ds(step, ROWS, stride=STEPS)
            q = pf[a, rows, :]
            fresh = [
                jnp.sum(
                    q * pf[PER_GROUP, pl.ds(u, ROWS, stride=STEPS), :], axis=1, keepdims=True
                )
                * SCALE
                for u in range(step + 1)
            ]
            tops = jnp.where(of_row[...] > 0.5, m_all[pl.ds(h, 1), :], -jnp.inf)
            top = jnp.max(tops, axis=1, keepdims=True)
            for s in fresh:
                top = jnp.maximum(top, s)
            share = jnp.exp(tops - top)
            total = jnp.sum(share * l_all[pl.ds(h, 1), :], axis=1, keepdims=True)
            out = jnp.dot(
                share, o_pg[pl.ds(h, PAGES, stride=32), :],
                preferred_element_type=jnp.float32, precision=lax.Precision.HIGHEST,
            )
            for u, s in enumerate(fresh):
                p = jnp.exp(s - top)
                total = total + p
                out = out + p * pf[PER_GROUP + 1, pl.ds(u, ROWS, stride=STEPS), :]
            joined[a, rows, :] = out / total
        return 0

    lax.fori_loop(0, PER_GROUP, head, 0)


class Place:
    def __init__(self):
        g, t = lax.axis_index("grp"), lax.axis_index("tp")
        self.g, self.t = g, t
        self.core = g % 2
        self.z = (g // 2) % 4
        self.yh = g // 8
        self.yl = t // 4
        self.x = t % 4
        self.y = self.yh * 2 + self.yl
        self.zm = (self.z + 3) % 4
        self.zp = (self.z + 1) % 4
        self.z2 = (self.z + 2) % 4

    def at(self, y=None, z=None, x=None, core=None):
        y = self.y if y is None else y
        z = self.z if z is None else z
        x = self.x if x is None else x
        core = self.core if core is None else core
        return ((y // 2) * 4 + z) * 2 + core, (y % 2) * 4 + x


def greet(me):
    barrier = pltpu.get_barrier_semaphore()

    def signal(who):
        pl.semaphore_signal(barrier, inc=1, device_id=who, device_id_type=MESH)

    def plane(k, _):
        signal(me.at(y=(me.y + k // 4) % 4, x=(me.x + k) % 4))
        return 0

    lax.fori_loop(1, 16, plane, 0)
    signal(me.at(z=me.zp))
    signal(me.at(z=me.zm))
    for k in range(4):
        signal(me.at(y=(me.y + k) % 4, core=1 - me.core))
    for k in range(1, 4):
        signal(me.at(x=(me.x + k) % 4, core=1 - me.core))
    pl.semaphore_wait(barrier, 24)


def remote(src, dst, sent, got, who):
    return pltpu.make_async_remote_copy(
        src, dst, sent, got, device_id=who, device_id_type=MESH
    )


class Ring:
    def __init__(self, me, count, order, slot, up, down, got):
        self.me, self.count, self.order, self.slot = me, count, order, slot
        self.up, self.down, self.got = up, down, got

    def send_up(self, z, p, k):
        return remote(
            self.slot(z, p), self.slot(z, p), self.up.at[k], self.got.at[z, p],
            self.me.at(z=self.me.zp),
        )

    def send_down(self, z, p, k):
        return remote(
            self.slot(z, p), self.slot(z, p), self.down.at[k], self.got.at[z, p],
            self.me.at(z=self.me.zm),
        )

    def arrived(self, z, p):
        self.send_up(z, p, 0).wait_recv()

    def send(self, k):
        p = self.order(k)
        self.send_up(self.me.z, p, k).start()
        self.send_down(self.me.z, p, k).start()

    def pass_local(self, local):
        for k, copy in enumerate(local):
            copy.wait()
            self.send(k)

    def pass_own(self, low):
        def one(k, _):
            self.arrived(self.me.z, self.order(k))
            self.send(k)
            return 0

        lax.fori_loop(low, self.count, one, 0)

    def pass_on(self, low, high):
        me = self.me

        def two(n, _):
            p, q = self.order(2 * n), self.order(2 * n + 1)
            self.arrived(me.zm, p)
            self.send_up(me.zm, p, self.count + n).start()
            self.arrived(me.zp, p)
            self.arrived(me.zp, q)
            self.send_down(me.zp, q, self.count + n).start()
            self.arrived(me.zm, q)
            return 0

        lax.fori_loop(low, high, two, 0)

    def last(self, low, high):
        def one(k, _):
            self.arrived(self.me.z2, self.order(k))
            return 0

        lax.fori_loop(low, high, one, 0)

    def finish(self):
        def one(k, _):
            p = k % self.count
            self.send_up(self.me.z, p, k).wait_send()
            self.send_down(self.me.z, p, k).wait_send()
            return 0

        lax.fori_loop(0, self.count + self.count // 2, one, 0)


def ring_sems(count):
    dma = pltpu.SemaphoreType.DMA
    more = count + count // 2
    return [dma((count,)), dma((more,)), dma((more,)), dma((4, count))]


def layer_kernel(
    row_pages, last_fill, order, tok, w_qkv, w_out, cache_hbm, out,
    xbuf, qbuf, obuf, acc, squares, half_sent, half_got, full_sent, full_got,
    sq_half, sq_sum, sq_full,
    cache, pf, of_page, of_row, valid, q_pg, m_all, l_all, o_pg, joined,
    mine, ctx, o_acc, keep, give, taken, sums, final,
    own_sem, cache_sem,
    q_sent, q_up, q_down, q_got,
    w_sent, w_up, w_down, w_got, v_sent,
    x_sent, x_up, x_down, x_got,
    sq_s, sq_g, h_s, h_g, f_s, f_g,
    c_up, c_down, c_core, c_got,
    y_s, y_g, e_s, e_g,
):
    me = Place()
    c = me.core
    other = me.at(core=1 - c)
    right, left = me.at(x=(me.x + 1) % 4), me.at(x=(me.x + 3) % 4)
    xl, xr, x2 = (me.x + 3) % 4, (me.x + 1) % 4, (me.x + 2) % 4
    far = me.at(y=(me.y + 2) % 4)
    near = me.at(y=me.yh * 2 + 1 - me.yl)
    greet(me)

    piece = me.yh * 2 + c

    def half(h):
        return tok.at[:, pl.ds(pl.multiple_of(h * 512, 512), 512)]

    def x_first(n):
        h = (c + n % 2) % 2
        who = me.at(y=me.yl * 2 + (me.yl + n // 2) % 2, core=h)
        return remote(half(h), xbuf.at[me.x, piece], x_sent.at[n], x_got.at[me.x, piece], who)

    stays = me.yh == me.yl

    x_here = pltpu.make_async_copy(half(c), xbuf.at[me.x, piece], own_sem.at[0])

    @pl.when(stays)
    def _():
        x_here.start()

    @pl.when(jnp.logical_not(stays))
    def _():
        x_first(0).start()

    for n in range(1, 4):
        x_first(n).start()

    def q_columns(t):
        return w_qkv.at[:, pl.ds(pl.multiple_of(t * QC, QC), QC)]

    def q_plane(k):
        t = (me.t + k) % TP
        return remote(q_columns(t), qbuf.at[me.z, me.t], q_sent.at[k], q_got.at[me.z, me.t], (me.g, t))

    def q_start(k, _):
        q_plane(k).start()
        return 0

    q_here = [pltpu.make_async_copy(q_columns(me.t), qbuf.at[me.z, me.t], own_sem.at[1])]
    q_here[0].start()
    lax.fori_loop(1, TP, q_start, 0)
    q_ring = Ring(
        me, TP, lambda k: (me.t + TP - k) % TP, lambda z, p: qbuf.at[z, p], q_up, q_down, q_got
    )

    q_ring.pass_local(q_here)

    def cached(n):
        rows = pl.ds(n * 16, 16)
        return pltpu.make_async_copy(cache_hbm.at[rows], cache.at[rows], cache_sem.at[n])

    for n in range(8):
        cached(n).start()

    def x_along(x, p, who, sem):
        return remote(xbuf.at[x, p], xbuf.at[x, p], sem, x_got.at[x, p], who)

    for n in range(4):
        p = (piece + n) % 4
        if n:
            x_along(me.x, p, right, x_up.at[0]).wait_recv()
        else:

            @pl.when(stays)
            def _():
                x_here.wait()

            @pl.when(jnp.logical_not(stays))
            def _():
                x_along(me.x, piece, right, x_up.at[0]).wait_recv()

        x_along(me.x, p, right, x_up.at[n]).start()
        x_along(me.x, p, left, x_down.at[n]).start()

    def w_columns(yl, n):
        return w_out.at[:, pl.ds(pl.multiple_of((yl * 4 + n) * OC, OC), OC)]

    def w_slot(z, p):
        return obuf.at[z, p // 4, p % 4]

    def w_plane(k):
        y = jnp.where(k == 4, me.yh * 2 + 1 - me.yl, (me.y + 1 + (k - 5) // 3) % 4)
        n = jnp.where(k == 4, 3, (k - 5) % 3)
        p = me.y * 4 + n
        return remote(w_columns(y % 2, n), w_slot(me.z, p), w_sent.at[k], w_got.at[me.z, p], me.at(y=y))

    def w_order(k):
        first = me.y * 4 + (k + 3) % 4
        later = ((me.y + 3 - (k - 5) // 3) % 4) * 4 + (k - 5) % 3
        swap = (me.yh * 2 + 1 - me.yl) * 4 + 3
        return jnp.where(k < 4, first, jnp.where(k == 4, swap, later))

    def w_far(j, m):
        z, p = (me.z + j) % 4, (me.yh * 2 + m) * 4 + 3
        return remote(w_slot(z, p), w_slot(z, p), v_sent.at[j, m], w_got.at[z, p], far)

    def w_cross(j):
        for m in range(2):
            w_far(j, m).start()

    def w_crossed(j):
        for m in range(2):
            w_ring.arrived((me.z + j) % 4, ((1 - me.yh) * 2 + m) * 4 + 3)

    def w_start(k, _):
        w_plane(k).start()
        return 0

    w_here = [
        pltpu.make_async_copy(w_columns(me.yl, n), w_slot(me.z, me.y * 4 + n), own_sem.at[2 + n])
        for n in (3, 0, 1, 2)
    ]
    for copy in w_here:
        copy.start()
    lax.fori_loop(4, 14, w_start, 0)
    w_ring = Ring(
        me, 14, w_order, w_slot, w_up, w_down, w_got
    )


    def square(x, fresh=False):
        def part(n, _):
            p, at = n // 4, pl.ds(pl.multiple_of((n % 4) * 64, 64), 64)
            v = xbuf[x, p, at, :].astype(jnp.float32)
            v = v * v
            v = v[:, :128] + v[:, 128:256] + v[:, 256:384] + v[:, 384:]
            squares[p, at, :] = v if fresh else squares[p, at, :] + v
            return 0

        lax.fori_loop(0, 16, part, 0)

    square(me.x, True)
    page_maps(row_pages, last_fill, order, of_page, of_row, valid)
    q_ring.pass_own(1)
    for n in range(4):
        x_along(xl, n, right, x_up.at[0]).wait_recv()
        x_along(xr, n, right, x_up.at[0]).wait_recv()
        if n < 2:
            x_along(xl, n, right, x_up.at[4 + n]).start()
        else:
            x_along(xr, n, left, x_down.at[2 + n]).start()
    q_ring.pass_on(0, 4)
    w_ring.pass_local(w_here)
    w_ring.pass_own(4)
    w_cross(0)

    def product(z, n):
        cols = pl.ds(pl.multiple_of(n * 256, 256), 256)
        xs = xbuf[z].reshape(4 * TOK, 512)
        ws = qbuf[z, :, :, cols].reshape(512, 256)
        return cols, jnp.dot(xs, ws, preferred_element_type=jnp.float32)

    def multiply(z, fresh=False):
        def tile(n, _):
            cols, value = product(z, n)
            acc[:, cols] = value if fresh else acc[:, cols] + value
            return 0

        lax.fori_loop(0, QC // 256, tile, 0)

    gap = (me.z2 + 4 - x2) % 4
    one = (x2 + jnp.where(gap == 1, 2, 1)) % 4
    two = (x2 + jnp.where((gap == 0) | (gap == 3), 2, 3)) % 4
    three = jnp.where(gap == 0, (x2 + 3) % 4, x2)
    four = me.z2
    multiply(one, True)
    square(xl)
    square(xr)
    multiply(two)
    for n in range(4):
        x_along(x2, n, right, x_up.at[0]).wait_recv()
    square(x2)
    sq_swap = [
        remote(squares.at[2 * n + 1 - c], sq_half.at[n], sq_s.at[n], sq_g.at[n], other)
        for n in range(2)
    ]
    for copy in sq_swap:
        copy.start()
    multiply(three)
    for copy in sq_swap:
        copy.wait_recv()
    for n in range(2):
        sq_sum[n] = squares[2 * n + c] + sq_half[n]
    sq_far = remote(sq_sum.at[1 - me.yh], sq_full, sq_s.at[2], sq_g.at[2], far)
    sq_far.start()
    q_ring.last(0, TP)

    def half_copy(n):
        return remote(half_sent.at[n], half_got.at[n], h_s.at[n], h_g.at[n], other)

    def full_copy(n):
        return remote(full_sent.at[n], full_got.at[n], f_s.at[n], f_g.at[n], far)

    def block(p):
        return pl.ds(pl.multiple_of(p * TOK, TOK), TOK)

    def last_tile(n):
        cols, value = product(four, n)
        acc[:, cols] += value
        for m in range(2):
            half_sent[n, m] = acc[block(2 * m + 1 - c), cols].astype(jnp.bfloat16)
        half_copy(n).start()

    for n in range(QC // 256):
        last_tile(n)

    def join_half(n):
        cols = pl.ds(pl.multiple_of(n * 256, 256), 256)
        half_copy(n).wait_recv()
        theirs = acc[block(2 * (1 - me.yh) + c), cols] + half_got[n, 1 - me.yh].astype(jnp.float32)
        full_sent[n] = theirs.astype(jnp.bfloat16)
        full_copy(n).start()
        acc[block(piece), cols] += half_got[n, me.yh].astype(jnp.float32)

    for n in range(QC // 256):
        join_half(n)
    w_ring.pass_on(0, 4)
    w_cross(1)
    w_cross(3)
    sq_far.wait_recv()
    mean = jnp.sum(sq_sum[me.yh] + sq_full[...], axis=1, keepdims=True) * (1.0 / D)
    gain = lax.rsqrt(mean + EPS)

    def join_full(n):
        cols = pl.ds(pl.multiple_of(n * 256, 256), 256)
        full_copy(n).wait_recv()
        total = acc[block(piece), cols] + full_got[n].astype(jnp.float32)
        total = (total * gain).astype(jnp.bfloat16).astype(jnp.float32)
        pf[2 * n], pf[2 * n + 1] = total[:, :HD], total[:, HD:]

    for n in range(QC // 256):
        join_full(n)

    page_queries(pf, of_page, q_pg)
    for n in range(8):
        cached(n).wait()
    cached_tokens(cache, q_pg, valid, m_all, l_all, o_pg)
    join_pages(pf, of_row, m_all, l_all, o_pg, joined)
    for a in range(PER_GROUP):
        mine[:, pl.ds(a * HD, HD)] = joined[a].astype(jnp.bfloat16)

    def c_along(x, core, h, sem, who):
        slot = ctx.at[x, core, h]
        return remote(slot, slot, sem, c_got.at[x, core, h], who)

    def c_first(h, sem, who):
        slot = ctx.at[me.x, c, h]
        return remote(mine.at[pl.ds(h * 128, 128)], slot, sem, c_got.at[me.x, c, h], who)

    c_here = [
        pltpu.make_async_copy(
            mine.at[pl.ds(h * 128, 128)], ctx.at[me.x, c, h], own_sem.at[6 + h]
        )
        for h in range(2)
    ]
    for h in range(2):
        c_first(h, c_up.at[h], right).start()
        c_first(h, c_down.at[h], left).start()
        c_first(h, c_core.at[h], other).start()
        c_here[h].start()
    w_ring.pass_on(4, 7)
    w_ring.arrived(me.z2, w_order(0))
    w_ring.arrived(me.z2, w_order(4))
    w_cross(2)
    for h in range(2):
        c_along(xl, c, h, c_up.at[0], right).wait_recv()
        if h == 0:
            c_along(xl, c, h, c_up.at[2], right).start()
        c_along(xl, c, h, c_core.at[2 + h], other).start()
        c_along(xr, c, h, c_up.at[0], right).wait_recv()
        if h == 1:
            c_along(xr, c, h, c_down.at[2], left).start()
        c_along(xr, c, h, c_core.at[4 + h], other).start()

    def from_other(x):
        for h in range(2):
            c_along(x, 1 - c, h, c_up.at[0], right).wait_recv()

    def y_copy(j):
        return remote(give.at[j], taken.at[j], y_s.at[j], y_g.at[j], near)

    def term(j, n, fresh=False):
        ws = obuf[(me.z + j) % 4, :, n].reshape(256, OC)
        xs = ctx[n].reshape(2 * TOK, OC)
        value = lax.dot_general(
            xs, ws, (((1,), (1,)), ((), ())), preferred_element_type=jnp.float32
        )
        o_acc[j] = value if fresh else o_acc[j] + value

    def terms(n, fresh=False):
        def some(m, _):
            term((m + 3) % 4, n, fresh)
            return 0

        lax.fori_loop(0, 3, some, 0)

    def hand_over(j):
        keep[j] = o_acc[j, :, pl.ds(pl.multiple_of(me.yl * 128, 128), 128)]
        theirs = o_acc[j, :, pl.ds(pl.multiple_of((1 - me.yl) * 128, 128), 128)]
        give[j] = theirs.astype(jnp.bfloat16)
        y_copy(j).start()

    for copy in c_here:
        copy.wait()
    from_other(me.x)
    for j in (0, 1, 3):
        w_crossed(j)
    terms(me.x, True)
    from_other(xl)
    terms(xl)
    from_other(xr)
    terms(xr)
    for h in range(2):
        c_along(x2, c, h, c_up.at[0], right).wait_recv()
        c_along(x2, c, h, c_core.at[6 + h], other).start()
    from_other(x2)
    for j in (0, 1, 3):
        term(j, x2)
        hand_over(j)

    def e_copy(j, z, m):
        core = (c + m) % 2
        return remote(
            sums.at[j, core], final.at[c, me.x], e_s.at[j, m], e_g.at[c, me.x], me.at(x=z, core=core)
        )

    def spread(j, z):
        y_copy(j).wait_recv()
        total = keep[j] + taken[j].astype(jnp.float32)
        sums[j] = total.astype(jnp.bfloat16).reshape(2, TOK, 128)
        e_copy(j, z, 1).start()

        @pl.when(z != me.x)
        def _():
            e_copy(j, z, 0).start()

        @pl.when(z == me.x)
        def _():
            here = pltpu.make_async_copy(sums.at[j, c], final.at[c, me.x], own_sem.at[8])
            here.start()
            here.wait()

    places = [(me.z + j) % 4 for j in range(4)]
    for j in (0, 1, 3):
        spread(j, places[j])
    w_ring.last(1, 4)
    w_ring.last(5, 14)
    w_crossed(2)
    term(2, 0, True)

    def rest(n, _):
        term(2, n)
        return 0

    lax.fori_loop(1, 4, rest, 0)
    hand_over(2)
    for j in (2,):
        spread(j, places[j])

    @pl.when(jnp.logical_not(stays))
    def _():
        x_first(0).wait_send()

    for n in range(1, 4):
        x_first(n).wait_send()
    for n in range(6):
        x_along(me.x, 0, right, x_up.at[n]).wait_send()
        x_along(me.x, 0, left, x_down.at[n]).wait_send()

    def q_done(k, _):
        q_plane(k).wait_send()
        return 0

    def w_done(k, _):
        w_plane(k).wait_send()
        return 0

    lax.fori_loop(1, TP, q_done, 0)
    lax.fori_loop(4, 14, w_done, 0)
    for j in range(4):
        for m in range(2):
            w_far(j, m).wait_send()
    q_ring.finish()
    w_ring.finish()
    for copy in sq_swap:
        copy.wait_send()
    sq_far.wait_send()
    for n in range(QC // 256):
        half_copy(n).wait_send()
        full_copy(n).wait_send()
    for n in range(3):
        c_along(me.x, c, 0, c_up.at[n], right).wait_send()
        c_along(me.x, c, 0, c_down.at[n], left).wait_send()
    for n in range(8):
        c_along(me.x, c, 0, c_core.at[n], other).wait_send()
    for j, z in enumerate(places):
        y_copy(j).wait_send()
        e_copy(j, z, 1).wait_send()

        @pl.when(z != me.x)
        def _(j=j, z=z):
            e_copy(j, z, 0).wait_send()

    for k in range(8):
        core, x = (c + k // 4) % 2, (me.x + k) % 4
        if k:
            remote(final.at[core, x], final.at[core, x], e_s.at[0, 0], e_g.at[core, x], other).wait_recv()

    for core in range(2):
        for yl in range(2):
            out[:, pl.ds(core * 512 + yl * 256, 256)] = jnp.concatenate(
                [final[core, x, :, pl.ds(yl * 64, 64)] for x in range(4)], axis=1
            )


def layer(row_pages, last_fill, order, tokens, w_qkv, w_out, cache):
    dma = pltpu.SemaphoreType.DMA
    inside = pl.BlockSpec(memory_space=pltpu.VMEM)
    anywhere = pl.BlockSpec(memory_space=pl.ANY)
    f32, bf16 = jnp.float32, jnp.bfloat16
    tiles = QC // 256

    def vmem(dtype, *shape):
        return pltpu.VMEM(shape, dtype)

    return pl.pallas_call(
        layer_kernel,
        out_shape=jax.ShapeDtypeStruct((TOK, OC), bf16),
        in_specs=[inside] * 3 + [anywhere] * 4,
        out_specs=pl.BlockSpec(memory_space=pltpu.VMEM),
        scratch_shapes=[
            vmem(bf16, 4, 4, TOK, 512),
            vmem(bf16, 4, TP, 64, QC),
            vmem(bf16, 4, 4, 4, 64, OC),
            vmem(f32, 4 * TOK, QC),
            vmem(f32, 4, TOK, 128),
            vmem(bf16, tiles, 2, TOK, 256),
            vmem(bf16, tiles, 2, TOK, 256),
            vmem(bf16, tiles, TOK, 256),
            vmem(bf16, tiles, TOK, 256),
            vmem(f32, 2, TOK, 128),
            vmem(f32, 2, TOK, 128),
            vmem(f32, TOK, 128),
            vmem(bf16, PAGES, 2 * BLOCK, HD),
            vmem(f32, PER_GROUP + 2, TOK, HD),
            vmem(f32, PAGES, PAGES),
            vmem(f32, ROWS, PAGES),
            vmem(f32, PAGES, PAGES),
            vmem(f32, PAGES * 32, HD),
            vmem(f32, 32, PAGES),
            vmem(f32, 32, PAGES),
            vmem(f32, PAGES * 32, HD),
            vmem(f32, PER_GROUP, TOK, HD),
            vmem(bf16, TOK, OC),
            vmem(bf16, 4, 2, 2, 128, OC),
            vmem(f32, 4, 2 * TOK, 256),
            vmem(f32, 4, 2 * TOK, 128),
            vmem(bf16, 4, 2 * TOK, 128),
            vmem(bf16, 4, 2 * TOK, 128),
            vmem(bf16, 4, 2, TOK, 128),
            vmem(bf16, 2, 4, TOK, 128),
            dma((9,)),
            dma((8,)),
        ]
        + ring_sems(TP)
        + [dma((14,)), dma((21,)), dma((21,)), dma((4, 16)), dma((4, 2))]
        + [dma((4,)), dma((6,)), dma((6,)), dma((4, 4))]
        + [dma((3,)), dma((3,)), dma((tiles,)), dma((tiles,)), dma((tiles,)), dma((tiles,))]
        + [dma((3,)), dma((3,)), dma((8,)), dma((4, 2, 2))]
        + [dma((4,)), dma((4,)), dma((4, 2)), dma((2, 4))],
        compiler_params=pltpu.CompilerParams(
            collective_id=0, has_side_effects=True, vmem_limit_bytes=60 * MIB
        ),
        cost_estimate=pl.CostEstimate(
            flops=2 * TOK * D * (QC + OC), bytes_accessed=16 * MIB, transcendentals=0
        ),
        name="layer",
    )(row_pages, last_fill, order, tokens, w_qkv, w_out, cache)


def per_device(tokens, w_qkv, w_out, kv_cache, row_pages, last_fill, page_order):
    mixed = layer(
        row_pages, last_fill, page_order,
        tokens.reshape(TOK, -1), w_qkv, w_out, kv_cache.reshape(PAGES, 2 * BLOCK, HD),
    )
    return mixed.reshape(ROWS, STEPS, -1)


def solution(mesh):
    placed = (
        P("grp", None, "tp"),
        P(("grp", "tp"), None),
        P(("grp", "tp"), None),
        P("grp", None, None, "tp"),
        P("grp", None),
        P("grp", None),
        P("grp", None),
    )
    return jax.shard_map(
        per_device, mesh=mesh, in_specs=placed, out_specs=P("grp", None, "tp"), check_vma=False
    )
```
